768 devices in a mesh: row: 96 (over y_hi, z, x), col: 8 (over y_lo, core).
Axes of the slice: x: 4, y: 8 (y_hi: 2, y_lo: 4; y = y_hi * 4 + y_lo), z: 12, core: 2. Of those that a mesh axis runs over, the one named last changes fastest.
Arguments:
- features: bfloat16 [8, 6144, 256], P('col', 'row'), may hold values from -6 to 6
- weight: bfloat16 [256, 256], replicated, may hold values from -0.375 to 0.375
- cotangent: bfloat16 [96, 512, 256], P('row', 'col'), may hold values from -6 to 6
- tile_values: bfloat16 [96, 8, 32, 128, 128], P('row', 'col'), may hold values from -0.21875 to 0.21875
- tile_rows: int32 [96, 8, 32], P('row', 'col'), may hold values from 0 to 3
- tile_cols: int32 [96, 8, 32], P('row', 'col'), may hold values from 0 to 47
- tile_count: int32 [96, 8], P('row', 'col'), may hold values from 8 to 32, as said below
Outputs:
- output: bfloat16 [96, 512, 256], P('row', 'col')
- grad_features: bfloat16 [8, 6144, 256], P('col', 'row')
- grad_weight: float32 [256, 256], replicated
The draws below stay inside these ranges and needn't reach their ends.
Inputs may be any that keep to these rules, and one draw needn't show every extreme that they name: `tile_count`: some grid block has all 32 slots live in every draw.
All inputs are finite; a program needn't handle non-finite values.
Results may differ from the reference program's by a relative error of at most 0.0063.
Values may be sent and summed in bfloat16 or wider, within the bound.
No kernel may reach another device: no remote copies, remote signals or barrier semaphores. Data moves between devices by JAX's collectives and lax.ppermute only.
A program may use at most 32 MiB of HBM per device.

```python
import jax
import jax.numpy as jnp
from jax import lax

F = 256
TILE = 128
SLOTS = 32
ROWNODES = 512
COLNODES = 6144
RT = 4
CT = 48
NODES = 49152
N_ROW = 96
N_COL = 8


def draw_tile_count(key, part):
    key = jax.random.fold_in(key, 7)
    key_base, key_heavy, key_pick, key_spot = jax.random.split(key, 4)
    base_count = jax.random.randint(key_base, (N_ROW, N_COL), SLOTS // 4, SLOTS // 2 + 1)
    heavy_count = jax.random.randint(key_heavy, (N_ROW, N_COL), 3 * SLOTS // 4, SLOTS + 1)
    picker = jax.random.randint(key_pick, (N_ROW, N_COL), 0, 16)
    counts = jnp.where(picker == 0, heavy_count, base_count).reshape(-1)
    spot_index = jax.random.randint(key_spot, (), 0, N_ROW * N_COL)
    counts = counts.at[spot_index].set(SLOTS)
    return counts.reshape(N_ROW, N_COL).astype(jnp.int32)


def set_ends(result, key, low, top_value):
    spot = [jax.random.randint(jax.random.fold_in(key, axis), (), 0, length) for axis, length in enumerate(result.shape)]
    main_axis = result.shape.index(max(result.shape))
    beside = spot[:main_axis] + [(spot[main_axis] + 1) % result.shape[main_axis]] + spot[main_axis + 1:]
    return result.at[tuple(spot)].set(low).at[tuple(beside)].set(top_value)


def block_scale(rng, shape, cuts, smallest, high):
    level = 1.0
    for axis_at, blocks in cuts:
        heights = jax.random.uniform(jax.random.fold_in(jax.random.fold_in(rng, 6), axis_at), (blocks,), jnp.float32, smallest / len(cuts), high / len(cuts))
        level = level * jnp.repeat(jnp.exp(heights), shape[axis_at] // blocks).reshape((-1,) + (1,) * (len(shape) - 1 - axis_at))
    return level


def normal_values(own_key, extent, width, bound, cuts=(), kind=jnp.bfloat16):
    level = block_scale(own_key, extent, cuts, -0.22, 0.18) if cuts else 1.0
    result = jax.random.normal(own_key, extent, jnp.float32) * width * level
    return jnp.minimum(jnp.maximum(result, -bound), bound).astype(kind)


def setup_inputs(seed: int = 0) -> dict:
    key_of = jax.random.split(jax.random.key(seed), 8)
    features = normal_values(key_of[0], (N_COL, COLNODES, F), 1.0, 6.0, ((0, 8), (1, 96)))
    weight = normal_values(key_of[1], (F, F), F ** -0.5, 0.375)
    cotangent = normal_values(key_of[2], (N_ROW, ROWNODES, F), 1.0, 6.0, ((0, 96), (1, 8)))
    tile_values = normal_values(key_of[3], (N_ROW, N_COL, SLOTS, TILE, TILE), (TILE * SLOTS // 5) ** -0.5, 0.21875, ((0, 96), (1, 8)))
    tile_rows = set_ends(jax.random.randint(key_of[4], (N_ROW, N_COL, SLOTS), 0, RT), jax.random.fold_in(key_of[4], 1), 0, RT - 1).astype(jnp.int32)
    tile_cols = set_ends(jax.random.randint(key_of[5], (N_ROW, N_COL, SLOTS), 0, CT), jax.random.fold_in(key_of[5], 1), 0, CT - 1).astype(jnp.int32)
    tile_count = draw_tile_count(jax.random.fold_in(key_of[7], 71), 0)
    return {"features": features, "weight": weight, "cotangent": cotangent, "tile_values": tile_values, "tile_rows": tile_rows, "tile_cols": tile_cols, "tile_count": tile_count}


def silu_slope(pre_act):
    sig = jax.nn.sigmoid(pre_act)
    return sig * (1.0 + pre_act * (1.0 - sig))


def reference(features, weight, cotangent, tile_values, tile_rows, tile_cols, tile_count):
    slot_ids = jnp.arange(SLOTS, dtype=jnp.int32)
    live_mask = (slot_ids[None, None, :] < tile_count[:, :, None]).astype(jnp.bfloat16)
    blocks = tile_values * live_mask[..., None, None]
    feat_tiles = features.reshape(N_COL, CT, TILE, F)
    col_range = jnp.arange(N_COL, dtype=jnp.int32)
    row_range = jnp.arange(N_ROW, dtype=jnp.int32)

    def forward_block(row_index):
        picked = feat_tiles[col_range[:, None], tile_cols[row_index]]
        products = jnp.einsum('csij,csjf->csif', blocks[row_index].astype(jnp.float32), picked.astype(jnp.float32))
        row_hot = (tile_rows[row_index][:, :, None] == jnp.arange(RT, dtype=jnp.int32)).astype(jnp.float32)
        spread = jnp.einsum('csr,csif->rif', row_hot, products, precision=lax.Precision.HIGHEST)
        return spread.reshape(ROWNODES, F)

    aggregated = lax.map(forward_block, row_range).astype(jnp.bfloat16)
    flat_agg = aggregated.reshape(NODES, F)
    pre_act = jnp.dot(flat_agg, weight, preferred_element_type=jnp.float32)
    output = jax.nn.silu(pre_act).astype(jnp.bfloat16)
    grad_pre = (cotangent.reshape(NODES, F).astype(jnp.float32) * silu_slope(pre_act)).astype(jnp.bfloat16)
    grad_weight = jnp.dot(flat_agg.T, grad_pre, preferred_element_type=jnp.float32) * (NODES ** -0.5)
    grad_agg = lax.dot_general(grad_pre, weight, (((1,), (1,)), ((), ())), preferred_element_type=jnp.float32).astype(jnp.bfloat16)
    grad_tiles = grad_agg.reshape(N_ROW, RT, TILE, F)

    def backward_block(col_index):
        picked = grad_tiles[row_range[:, None], tile_rows[:, col_index]]
        products = jnp.einsum('rsji,rsjf->rsif', blocks[:, col_index].astype(jnp.float32), picked.astype(jnp.float32))
        col_hot = (tile_cols[:, col_index][:, :, None] == jnp.arange(CT, dtype=jnp.int32)).astype(jnp.float32)
        spread = jnp.einsum('rsk,rsif->kif', col_hot, products, precision=lax.Precision.HIGHEST)
        return spread.reshape(COLNODES, F)

    grad_features = lax.map(backward_block, col_range).astype(jnp.bfloat16)
    return output.reshape(N_ROW, ROWNODES, F), grad_features, grad_weight
```

```python
import functools

import jax
import jax.numpy as jnp
from jax import lax
from jax.experimental import pallas as pl
from jax.experimental.pallas import tpu as pltpu
from jax.sharding import Mesh
from jax.sharding import PartitionSpec as P

BF = jnp.bfloat16
F32 = jnp.float32
TILE = 128
STRIP = 64
SPLIT = (2, 12, 4, 4, 2)
NAMES = ("yh", "z", "x", "yl", "core")
ROW = ("yh", "z", "x")
COL = ("yl", "core")
VMEM_LIMIT = 40 * 1024 * 1024


def spec(space):
    return pl.BlockSpec(memory_space=space)


def pack_kernel(info, tiles, cot, meta, same, other):
    slots = tiles.shape[0]
    odd = info[0] == 1

    def one(s, carry):
        turned = tiles[s].T
        low, high = turned[:STRIP], turned[STRIP:]
        same[s] = jnp.where(odd, high, low)
        other[s] = jnp.where(odd, low, high)
        return carry

    lax.fori_loop(0, slots, one, 0, unroll=4)
    for ref in (same, other):
        ref[slots] = cot[:, :TILE]
        ref[slots + 1] = cot[:, TILE:]
        ref[slots + 2] = jnp.broadcast_to(meta[...], (STRIP, TILE)).astype(BF)


def fwd_kernel(slots, nz, codes, info, s0, s1, s2, s3, feats, o0, o1, o2, o3, acc):
    rows = o0.shape[0]
    mine, my_yh = info[1], info[2]
    acc[...] = jnp.zeros_like(acc)
    for j, strips in enumerate((s0, s1, s2, s3)):

        def one(s, carry, j=j, strips=strips):
            code = codes[j, s]
            col, row = code >> 2, code & 3

            @pl.when((code >= 0) & ((col & 1) == mine))
            def _():
                q = col >> 1
                far = (q >= nz).astype(jnp.int32)
                place = (q - far * nz) * 2 + (far ^ my_yh)
                block = feats[pl.ds(pl.multiple_of(place * STRIP, STRIP), STRIP), :]
                term = lax.dot_general(strips[s], block, (((0,), (0,)), ((), ())), preferred_element_type=F32)
                at = pl.ds(pl.multiple_of(j * rows + row * TILE, TILE), TILE)
                acc[at, :] = acc[at, :] + term

            return carry

        lax.fori_loop(0, slots, one, 0)
    for j, ref in enumerate((o0, o1, o2, o3)):
        ref[...] = acc[j * rows : (j + 1) * rows, :].astype(ref.dtype)


def bwd_kernel(slots, codes, info, s0, s1, s2, s3, a0, a1, a2, a3, cot, w, out, chunks, ga, acc, gw, act):
    rows, feat = a0.shape
    mine, col_pos = info[1], info[3]
    share = feat // cot.shape[0]
    acc[...] = jnp.zeros_like(acc)
    for j, agg in enumerate((a0, a1, a2, a3)):
        pre = jnp.dot(agg[...], w[...], preferred_element_type=F32)
        sig = jax.nn.sigmoid(pre)
        if j == 0:
            act[...] = pre * sig
        slope = sig * (1.0 + pre * (1.0 - sig))
        cot_j = cot[:, j].reshape(rows, feat).astype(F32)
        gp = (cot_j * slope).astype(BF)
        term = lax.dot_general(agg[...], gp, (((0,), (0,)), ((), ())), preferred_element_type=F32)
        gw[...] = term if j == 0 else gw[...] + term
        ga[j * rows : (j + 1) * rows, :] = lax.dot_general(
            gp, w[...], (((1,), (1,)), ((), ())), preferred_element_type=F32
        ).astype(BF)
    out[...] = act[pl.ds(pl.multiple_of(col_pos * STRIP, STRIP), STRIP), :].astype(BF)
    for j, strips in enumerate((s0, s1, s2, s3)):

        def one(s, carry, j=j, strips=strips):
            code = codes[j, s]
            col, row = code >> 2, code & 3

            @pl.when((code >= 0) & ((col & 1) == mine))
            def _():
                block = ga[pl.ds(pl.multiple_of(j * rows + row * TILE, TILE), TILE), :]
                term = jnp.dot(strips[s], block, preferred_element_type=F32)
                at = pl.ds(pl.multiple_of((col >> 1) * STRIP, STRIP), STRIP)
                acc[at, :] = acc[at, :] + term

            return carry

        lax.fori_loop(0, slots, one, 0)
    part = gw[pl.ds(pl.multiple_of(col_pos * share, share), share), :].astype(BF)
    for q in range(chunks.shape[0]):
        chunks[q, :STRIP, :] = acc[q * STRIP : (q + 1) * STRIP, :].astype(BF)
        chunks[q, STRIP:, :] = part


def shift(value, axis, by):
    n = lax.axis_size(axis)
    return lax.ppermute(value, axis, [(i, (i + by) % n) for i in range(n)])


def on_device(features, weight, cotangent, tile_values, tile_rows, tile_cols, tile_count):
    own = features[0]
    per_dev, feat = own.shape
    slots = tile_values.shape[2]
    nz = lax.axis_size("z")
    groups = 2 * nz
    col_devs = lax.axis_size(COL)
    rows = per_dev * col_devs
    x = lax.axis_index("x")
    share = feat // col_devs
    info = jnp.stack([x % 2, x // 2, lax.axis_index("yh"), lax.axis_index(COL)]).astype(jnp.int32)
    params = pltpu.CompilerParams(vmem_limit_bytes=VMEM_LIMIT)
    vmem, smem = spec(pltpu.VMEM), spec(pltpu.SMEM)

    live = jnp.arange(slots, dtype=jnp.int32) < tile_count[0, 0]
    code = jnp.where(live, tile_rows[0, 0] + 4 * tile_cols[0, 0], -1)
    meta = jnp.pad(code.astype(F32), (0, TILE - slots))[None]

    facing = shift(own, "yh", 1)
    near = jnp.concatenate([own, facing], axis=0)

    parcel = jax.ShapeDtypeStruct((slots + 3, STRIP, TILE), BF)
    same, other = pl.pallas_call(
        pack_kernel,
        out_shape=(parcel, parcel),
        in_specs=[smem, vmem, vmem, vmem],
        out_specs=(vmem, vmem),
        compiler_params=params,
        name="pack",
    )(info, tile_values[0, 0], cotangent[0], meta)
    strips = [same] + [shift(same if d == 2 else other, "x", d) for d in (1, 2, 3)]

    column = lax.all_gather(near, "z", axis=0, tiled=True)

    codes = jnp.stack([code] + [s[slots + 2, 0, :slots].astype(jnp.int32) for s in strips[1:]])
    cots = jnp.stack([jnp.concatenate([s[slots], s[slots + 1]], axis=1) for s in strips])
    cot_all = lax.all_gather(cots.reshape(4 * STRIP, feat), COL, axis=0, tiled=True)
    cot_all = cot_all.reshape(col_devs, 4, STRIP, feat)

    half = jax.ShapeDtypeStruct((rows, feat), BF)
    parts = pl.pallas_call(
        functools.partial(fwd_kernel, slots, nz),
        out_shape=(jax.ShapeDtypeStruct((rows, feat), F32), half, half, half),
        in_specs=[smem, smem] + [vmem] * 5,
        out_specs=(vmem,) * 4,
        scratch_shapes=[pltpu.VMEM((4 * rows, feat), F32)],
        compiler_params=params,
        name="forward_tiles",
    )(codes, info, *strips, column)

    back = [shift(parts[d], "x", -d) for d in (1, 2, 3)]
    block_sum = (parts[0] + (back[0].astype(F32) + back[1].astype(F32) + back[2].astype(F32))).astype(BF)
    pieces = lax.all_to_all(block_sum, COL, split_axis=0, concat_axis=0, tiled=True)
    agg = jnp.sum(pieces.reshape(col_devs, per_dev, feat).astype(F32), axis=0).astype(BF)
    block_agg = lax.all_gather(agg, COL, axis=0, tiled=True)
    aggs = [block_agg] + [shift(block_agg, "x", d) for d in (1, 2, 3)]

    output_rows, chunks = pl.pallas_call(
        functools.partial(bwd_kernel, slots),
        out_shape=(
            jax.ShapeDtypeStruct((per_dev, feat), BF),
            jax.ShapeDtypeStruct((groups, STRIP + share, feat), BF),
        ),
        in_specs=[smem, smem] + [vmem] * 10,
        out_specs=(vmem, vmem),
        scratch_shapes=[
            pltpu.VMEM((4 * rows, feat), BF),
            pltpu.VMEM((groups * STRIP, feat), F32),
            pltpu.VMEM((feat, feat), F32),
            pltpu.VMEM((rows, feat), F32),
        ],
        compiler_params=params,
        name="backward_tiles",
    )(codes, info, *strips, *aggs, cot_all, weight)

    arrived = lax.all_to_all(chunks, ("yh", "z"), split_axis=0, concat_axis=0, tiled=True)
    total = jnp.sum(arrived.astype(F32), axis=0)
    node_total = per_dev * lax.axis_size(ROW) * col_devs
    grad_weight = lax.all_gather(total[STRIP:] * node_total ** (-0.5), COL, axis=0, tiled=True)
    return output_rows[None], total[:STRIP].astype(BF)[None], grad_weight


def build(mesh, split):
    grid = Mesh(mesh.devices.reshape(split), NAMES)
    return jax.shard_map(
        on_device,
        mesh=grid,
        in_specs=(
            P(COL, ROW, None),
            P(),
            P(ROW, COL, None),
            P(ROW, COL, None, None, None),
            P(ROW, COL, None),
            P(ROW, COL, None),
            P(ROW, COL),
        ),
        out_specs=(P(ROW, COL, None), P(COL, ROW, None), P()),
        check_vma=False,
    )


def solution(mesh):
    return build(mesh, SPLIT)
```

```python
import functools

import jax
import jax.numpy as jnp
from jax import lax
from jax.experimental import pallas as pl
from jax.experimental.pallas import tpu as pltpu
from jax.sharding import Mesh
from jax.sharding import PartitionSpec as P

BF = jnp.bfloat16
F32 = jnp.float32
TILE = 128
STRIP = 64
SPLIT = (2, 12, 4, 4, 2)
NAMES = ("yh", "z", "x", "yl", "core")
ROW = ("yh", "z", "x")
COL = ("yl", "core")
VMEM_LIMIT = 40 * 1024 * 1024


def spec(space):
    return pl.BlockSpec(memory_space=space)


def pack_kernel(info, tiles, cot, meta, same, other):
    slots = tiles.shape[0]
    odd = info[0] == 1

    def one(s, carry):
        turned = tiles[s].T
        low, high = turned[:STRIP], turned[STRIP:]
        same[s] = jnp.where(odd, high, low)
        other[s] = jnp.where(odd, low, high)
        return carry

    lax.fori_loop(0, slots, one, 0, unroll=4)
    for ref in (same, other):
        ref[slots] = cot[:, :TILE]
        ref[slots + 1] = cot[:, TILE:]
        ref[slots + 2] = jnp.broadcast_to(meta[...], (STRIP, TILE)).astype(BF)


def fwd_kernel(slots, nz, codes, info, places, s0, s1, s2, s3, f0, f1, f2, o0, o1, o2, o3, feats, acc):
    rows = o0.shape[0]
    mine, my_yh, my_z = info[1], info[2], info[4]
    acc[...] = jnp.zeros_like(acc)
    part = f0.shape[0]
    for i, ref in enumerate((f0, f1, f2)):
        feats[i * part : (i + 1) * part, :] = ref[...]
    for j, strips in enumerate((s0, s1, s2, s3)):

        def one(s, carry, j=j, strips=strips):
            code = codes[j, s]
            col, row = code >> 2, code & 3

            @pl.when((code >= 0) & ((col & 1) == mine))
            def _():
                q = col >> 1
                far = (q >= nz).astype(jnp.int32)
                away = q - far * nz - my_z
                away = jnp.where(away < 0, away + nz, away)
                place = places[away] * 2 + (far ^ my_yh)
                block = feats[pl.ds(pl.multiple_of(place * STRIP, STRIP), STRIP), :]
                term = lax.dot_general(strips[s], block, (((0,), (0,)), ((), ())), preferred_element_type=F32)
                at = pl.ds(pl.multiple_of(j * rows + row * TILE, TILE), TILE)
                acc[at, :] = acc[at, :] + term

            return carry

        lax.fori_loop(0, slots, one, 0)
    for j, ref in enumerate((o0, o1, o2, o3)):
        ref[...] = acc[j * rows : (j + 1) * rows, :].astype(ref.dtype)


def bwd_kernel(
    slots, nz, codes, info, s0, s1, s2, s3, a0, a1, a2, a3, cot, w, out, keep, up, down, ga, acc, gw4, gw, act
):
    rows, feat = a0.shape
    mine, my_yh, col_pos, my_z, my_x = info[1], info[2], info[3], info[4], info[5]
    third = gw.shape[0] // 3
    acc[...] = jnp.zeros_like(acc)
    for j, agg in enumerate((a0, a1, a2, a3)):
        pre = jnp.dot(agg[...], w[...], preferred_element_type=F32)
        sig = jax.nn.sigmoid(pre)
        if j == 0:
            act[...] = pre * sig
        slope = sig * (1.0 + pre * (1.0 - sig))
        cot_j = cot[:, j].reshape(rows, feat).astype(F32)
        gp = (cot_j * slope).astype(BF)
        gw4[(my_x - j) & 3] = lax.dot_general(agg[...], gp, (((0,), (0,)), ((), ())), preferred_element_type=F32)
        ga[j * rows : (j + 1) * rows, :] = lax.dot_general(
            gp, w[...], (((1,), (1,)), ((), ())), preferred_element_type=F32
        ).astype(BF)
    out[...] = act[pl.ds(pl.multiple_of(col_pos * STRIP, STRIP), STRIP), :].astype(BF)
    gw[:feat, :] = (gw4[0] + gw4[1]) + (gw4[2] + gw4[3])
    gw[feat:, :] = jnp.zeros((gw.shape[0] - feat, feat), F32)
    for j, strips in enumerate((s0, s1, s2, s3)):

        def one(s, carry, j=j, strips=strips):
            code = codes[j, s]
            col, row = code >> 2, code & 3

            @pl.when((code >= 0) & ((col & 1) == mine))
            def _():
                block = ga[pl.ds(pl.multiple_of(j * rows + row * TILE, TILE), TILE), :]
                term = jnp.dot(strips[s], block, preferred_element_type=F32)
                at = pl.ds(pl.multiple_of((col >> 1) * STRIP, STRIP), STRIP)
                acc[at, :] = acc[at, :] + term

            return carry

        lax.fori_loop(0, slots, one, 0)
    for base, ref in ((0, keep), (1, up), (-1, down)):
        for k, stride in enumerate((0, 3, -3, 6)):
            to_z = lax.rem(my_z + (base + stride + nz), nz)
            for i in range(2):
                q = (my_yh ^ i) * nz + to_z
                at = (2 * k + i) * STRIP
                ref[at : at + STRIP, :] = acc[pl.ds(pl.multiple_of(q * STRIP, STRIP), STRIP), :].astype(ref.dtype)
        which = lax.rem(my_z + (base + 3), 3)
        ref[8 * STRIP :, :] = gw[pl.ds(pl.multiple_of(which * third, third), third), :].astype(ref.dtype)


def near_kernel(keep, up, down, p1, p2, p3, own, weight_own):
    block = 2 * STRIP

    def total(lo, hi):
        return keep[lo:hi, :] + up[lo:hi, :].astype(F32) + down[lo:hi, :].astype(F32)

    tail = total(4 * block, keep.shape[0]).astype(BF)
    own[...] = total(0, block)
    weight_own[...] = tail
    for k, ref in enumerate((p1, p2, p3)):
        ref[:block, :] = total((k + 1) * block, (k + 2) * block).astype(BF)
        ref[block:, :] = tail


def far_kernel(info, own, weight_own, r1, r2, r3, send, keep, weight_sum, terms):
    block = 2 * STRIP
    group = lax.div(info[4], 3)
    total = own[...]
    terms[group] = weight_own[...].astype(F32)
    for ref, step in ((r1, 3), (r2, 1), (r3, 2)):
        total = total + ref[:block, :].astype(F32)
        terms[(group + step) & 3] = ref[block:, :].astype(F32)
    summed = ((terms[0] + terms[1]) + (terms[2] + terms[3])).astype(BF)
    keep[...] = total[:STRIP]
    send[:STRIP, :] = total[STRIP:].astype(BF)
    send[STRIP:, :] = summed
    weight_sum[...] = summed


def last_kernel(scale, keep, weight_sum, arrived, grads, weight_third):
    grads[...] = (keep[...] + arrived[:STRIP, :].astype(F32)).astype(BF)
    weight_third[...] = (weight_sum[...].astype(F32) + arrived[STRIP:, :].astype(F32)) * scale


def join_kernel(info, own, below, above, out, whole):
    third = own.shape[0]
    for ref, step in ((own, 0), (below, 2), (above, 1)):
        which = lax.rem(info[4] + step, 3)
        whole[pl.ds(pl.multiple_of(which * third, third), third), :] = ref[...]
    out[...] = whole[: out.shape[0], :]


def shift(value, axis, by):
    n = lax.axis_size(axis)
    return lax.ppermute(value, axis, [(i, (i + by) % n) for i in range(n)])


def on_device(features, weight, cotangent, tile_values, tile_rows, tile_cols, tile_count):
    own = features[0]
    per_dev, feat = own.shape
    slots = tile_values.shape[2]
    nz = lax.axis_size("z")
    groups = 2 * nz
    col_devs = lax.axis_size(COL)
    rows = per_dev * col_devs
    x, z = lax.axis_index("x"), lax.axis_index("z")
    info = jnp.stack([x % 2, x // 2, lax.axis_index("yh"), lax.axis_index(COL), z, x]).astype(jnp.int32)
    params = pltpu.CompilerParams(vmem_limit_bytes=VMEM_LIMIT)
    vmem, smem = spec(pltpu.VMEM), spec(pltpu.SMEM)

    def call(kernel, name, ins, outs, scratch, *args):
        return pl.pallas_call(
            kernel,
            out_shape=tuple(jax.ShapeDtypeStruct(s, t) for s, t in outs),
            in_specs=ins,
            out_specs=(vmem,) * len(outs),
            scratch_shapes=[pltpu.VMEM(s, t) for s, t in scratch],
            compiler_params=params,
            name=name,
        )(*args)

    live = jnp.arange(slots, dtype=jnp.int32) < tile_count[0, 0]
    code = jnp.where(live, tile_rows[0, 0] + 4 * tile_cols[0, 0], -1)
    meta = jnp.pad(code.astype(F32), (0, TILE - slots))[None]

    facing = shift(own, "yh", 1)
    near = jnp.concatenate([own, facing], axis=0)
    group = jnp.concatenate([near] + [shift(near, "z", d) for d in (3, -3, 6)], axis=0)
    below, above = shift(group, "z", 1), shift(group, "z", -1)
    places = jnp.array([0, 8, 6, 2, 10, 7, 3, 11, 5, 1, 9, 4], jnp.int32)

    parcel = ((slots + 3, STRIP, TILE), BF)
    same, other = call(
        pack_kernel, "pack", [smem, vmem, vmem, vmem], [parcel] * 2, [], info, tile_values[0, 0], cotangent[0], meta
    )
    strips = [same] + [shift(same if d == 2 else other, "x", d) for d in (1, 2, 3)]
    codes = jnp.stack([code] + [s[slots + 2, 0, :slots].astype(jnp.int32) for s in strips[1:]])
    cots = jnp.stack([jnp.concatenate([s[slots], s[slots + 1]], axis=1) for s in strips])
    cot_all = lax.all_gather(cots.reshape(4 * STRIP, feat), COL, axis=0, tiled=True)
    cot_all = cot_all.reshape(col_devs, 4, STRIP, feat)

    parts = call(
        functools.partial(fwd_kernel, slots, nz),
        "forward_tiles",
        [smem, smem, smem] + [vmem] * 7,
        [((rows, feat), F32)] + [((rows, feat), BF)] * 3,
        [((groups * STRIP, feat), BF), ((4 * rows, feat), F32)],
        codes, info, places, *strips, group, below, above,
    )

    back = [shift(parts[d], "x", -d) for d in (1, 2, 3)]
    block_sum = (parts[0] + (back[0].astype(F32) + back[1].astype(F32) + back[2].astype(F32))).astype(BF)
    pieces = lax.all_to_all(block_sum, COL, split_axis=0, concat_axis=0, tiled=True)
    agg = jnp.sum(pieces.reshape(col_devs, per_dev, feat).astype(F32), axis=0).astype(BF)
    block_agg = lax.all_gather(agg, COL, axis=0, tiled=True)
    aggs = [block_agg] + [shift(block_agg, "x", d) for d in (1, 2, 3)]

    third = -(-feat // 48) * 16
    group_rows = 8 * STRIP + third
    output_rows, keep, up, down = call(
        functools.partial(bwd_kernel, slots, nz),
        "backward_tiles",
        [smem, smem] + [vmem] * 10,
        [((per_dev, feat), BF), ((group_rows, feat), F32), ((group_rows, feat), BF), ((group_rows, feat), BF)],
        [
            ((4 * rows, feat), BF),
            ((groups * STRIP, feat), F32),
            ((4, feat, feat), F32),
            ((3 * third, feat), F32),
            ((rows, feat), F32),
        ],
        codes, info, *strips, *aggs, cot_all, weight,
    )

    message = ((2 * STRIP + third, feat), BF)
    p1, p2, p3, own_rows, weight_own = call(
        near_kernel,
        "near_sum",
        [vmem] * 3,
        [message] * 3 + [((2 * STRIP, feat), F32), ((third, feat), BF)],
        [],
        keep, shift(up, "z", 1), shift(down, "z", -1),
    )
    send, keep_rows, weight_sum = call(
        far_kernel,
        "far_sum",
        [smem] + [vmem] * 5,
        [((STRIP + third, feat), BF), ((STRIP, feat), F32), ((third, feat), BF)],
        [((4, third, feat), F32)],
        info, own_rows, weight_own, shift(p1, "z", 3), shift(p2, "z", -3), shift(p3, "z", 6),
    )
    node_total = per_dev * lax.axis_size(ROW) * col_devs
    grads, weight_third = call(
        functools.partial(last_kernel, node_total ** (-0.5)),
        "last_sum",
        [vmem] * 3,
        [((STRIP, feat), BF), ((third, feat), F32)],
        [],
        keep_rows, weight_sum, shift(send, "yh", 1),
    )
    (grad_weight,) = call(
        join_kernel,
        "join_weight",
        [smem] + [vmem] * 3,
        [((feat, feat), F32)],
        [((3 * third, feat), F32)],
        info, weight_third, shift(weight_third, "z", 1), shift(weight_third, "z", -1),
    )
    return output_rows[None], grads[None], grad_weight


def build(mesh, split):
    grid = Mesh(mesh.devices.reshape(split), NAMES)
    return jax.shard_map(
        on_device,
        mesh=grid,
        in_specs=(
            P(COL, ROW, None),
            P(),
            P(ROW, COL, None),
            P(ROW, COL, None, None, None),
            P(ROW, COL, None),
            P(ROW, COL, None),
            P(ROW, COL),
        ),
        out_specs=(P(ROW, COL, None), P(COL, ROW, None), P()),
        check_vma=False,
    )


def solution(mesh):
    return build(mesh, SPLIT)
```

```python
import functools

import jax
import jax.numpy as jnp
from jax import lax
from jax.experimental import pallas as pl
from jax.experimental.pallas import tpu as pltpu
from jax.sharding import Mesh
from jax.sharding import PartitionSpec as P

BF = jnp.bfloat16
F32 = jnp.float32
TILE = 128
STRIP = 64
SPLIT = (2, 4, 3, 4, 4, 2)
NAMES = ("yh", "za", "zb", "x", "yl", "core")
ROW = ("yh", "za", "zb", "x")
Z = ("za", "zb")
STEP = 4
COL = ("yl", "core")
VMEM_LIMIT = 40 * 1024 * 1024


def spec(space):
    return pl.BlockSpec(memory_space=space)


def pack_kernel(info, tiles, cot, meta, same, other):
    slots = tiles.shape[0]
    odd = info[0] == 1

    def one(s, carry):
        turned = tiles[s].T
        low, high = turned[:STRIP], turned[STRIP:]
        same[s] = jnp.where(odd, high, low)
        other[s] = jnp.where(odd, low, high)
        return carry

    lax.fori_loop(0, slots, one, 0, unroll=4)
    for ref in (same, other):
        ref[slots] = cot[:, :TILE]
        ref[slots + 1] = cot[:, TILE:]
        ref[slots + 2] = jnp.broadcast_to(meta[...], (STRIP, TILE)).astype(BF)


def live_list(codes, mine, place_of, table, strips, pool):
    slots = codes.shape[1]
    for j, ref in enumerate(strips):
        pool[j * slots : (j + 1) * slots] = ref[:slots]
    pool[4 * slots] = jnp.zeros((STRIP, TILE), BF)
    count = jnp.int32(0)
    for j in range(4):

        def one(s, n, j=j):
            code = codes[j, s]
            col, row = code >> 2, code & 3
            table[0, n] = j * slots + s
            table[1, n] = j * 4 + row
            table[2, n] = place_of(col >> 1)
            return n + ((code >= 0) & ((col & 1) == mine)).astype(jnp.int32)

        count = lax.fori_loop(0, slots, one, count, unroll=4)
    for i in range(STEP):
        table[0, count + i] = 4 * slots
        table[1, count + i] = 0
        table[2, count + i] = 0
    return count


def fwd_kernel(nz, codes, info, s0, s1, s2, s3, feats, o0, o1, o2, o3, table, pool, acc):
    rows = o0.shape[0]
    mine, my_yh = info[1], info[2]

    def place_of(q):
        far = (q >= nz).astype(jnp.int32)
        return (q - far * nz) * 2 + (far ^ my_yh)

    count = live_list(codes, mine, place_of, table, (s0, s1, s2, s3), pool)
    acc[...] = jnp.zeros_like(acc)

    def several(t, carry):
        terms = []
        for i in range(STEP):
            at = t * STEP + i
            block = feats[pl.ds(pl.multiple_of(table[2, at] * STRIP, STRIP), STRIP), :]
            term = lax.dot_general(
                pool[table[0, at]], block, (((0,), (0,)), ((), ())), preferred_element_type=F32
            )
            terms.append((pl.ds(pl.multiple_of(table[1, at] * TILE, TILE), TILE), term))
        for at, term in terms:
            acc[at, :] = acc[at, :] + term
        return carry

    lax.fori_loop(0, (count + (STEP - 1)) // STEP, several, 0)
    per = 4 * TILE
    for j, ref in enumerate((o0, o1, o2, o3)):
        ref[...] = acc[j * per : j * per + rows, :].astype(ref.dtype)


def bwd_kernel(
    nz, codes, info, s0, s1, s2, s3, a0, a1, a2, a3, cot, w, out, keep, up, down, table, pool, ga, acc, gw4, act
):
    rows, feat = a0.shape
    mine, col_pos, my_zb, my_x = info[1], info[3], info[4], info[5]
    share = feat // cot.shape[0]
    count = live_list(codes, mine, lambda q: q, table, (s0, s1, s2, s3), pool)
    acc[...] = jnp.zeros_like(acc)
    per = 4 * TILE
    for j, agg in enumerate((a0, a1, a2, a3)):
        pre = jnp.dot(agg[...], w[...], preferred_element_type=F32)
        sig = jax.nn.sigmoid(pre)
        if j == 0:
            act[...] = pre * sig
        slope = sig * (1.0 + pre * (1.0 - sig))
        cot_j = cot[:, j].reshape(rows, feat).astype(F32)
        gp = (cot_j * slope).astype(BF)
        gw4[(my_x - j) & 3] = lax.dot_general(agg[...], gp, (((0,), (0,)), ((), ())), preferred_element_type=F32)
        ga[j * per : j * per + rows, :] = lax.dot_general(
            gp, w[...], (((1,), (1,)), ((), ())), preferred_element_type=F32
        ).astype(BF)
    out[...] = act[pl.ds(pl.multiple_of(col_pos * STRIP, STRIP), STRIP), :].astype(BF)

    def several(t, carry):
        terms = []
        for i in range(STEP):
            at = t * STEP + i
            block = ga[pl.ds(pl.multiple_of(table[1, at] * TILE, TILE), TILE), :]
            term = jnp.dot(pool[table[0, at]], block, preferred_element_type=F32)
            terms.append((pl.ds(pl.multiple_of(table[2, at] * STRIP, STRIP), STRIP), term))
        for at, term in terms:
            acc[at, :] = acc[at, :] + term
        return carry

    lax.fori_loop(0, (count + (STEP - 1)) // STEP, several, 0)
    mine_rows = pl.ds(pl.multiple_of(col_pos * share, share), share)
    part = (gw4[0, mine_rows, :] + gw4[1, mine_rows, :]) + (gw4[2, mine_rows, :] + gw4[3, mine_rows, :])
    high = part.astype(BF)
    low = (part - high.astype(F32)).astype(BF)
    n_chunks = acc.shape[0] // (3 * STRIP)
    n_za = nz // 3
    for base, ref in ((0, keep), (1, up), (2, down)):
        which = lax.rem(my_zb + base, 3)
        for i in range(n_chunks):
            q = (i // n_za) * nz + 3 * (i % n_za) + which
            block = acc[pl.ds(pl.multiple_of(q * STRIP, STRIP), STRIP), :]
            ref[i * STRIP : (i + 1) * STRIP, :] = block.astype(ref.dtype)
    end = n_chunks * STRIP
    keep[end:, :] = part
    for ref in (up, down):
        ref[end : end + share, :] = high
        ref[end + share :, :] = low


def near_kernel(keep, up, down, chunks):
    n_chunks = chunks.shape[0]
    end = n_chunks * STRIP
    share = keep.shape[0] - end
    for i in range(n_chunks):
        at = slice(i * STRIP, (i + 1) * STRIP)
        chunks[i, :STRIP, :] = (keep[at, :] + (up[at, :].astype(F32) + down[at, :].astype(F32))).astype(BF)
    part = keep[end:, :]
    for ref in (up, down):
        part = part + (ref[end : end + share, :].astype(F32) + ref[end + share :, :].astype(F32))
    high = part.astype(BF)
    low = (part - high.astype(F32)).astype(BF)
    for i in range(n_chunks):
        chunks[i, STRIP : STRIP + share, :] = high
        chunks[i, STRIP + share :, :] = low


def far_kernel(scale, chunks, grads, weight_part):
    share = weight_part.shape[0]
    total = jnp.sum(chunks[...].astype(F32), axis=0)
    grads[...] = total[:STRIP].astype(BF)
    weight_part[...] = (total[STRIP : STRIP + share] + total[STRIP + share :]) * scale


def shift(value, axis, by):
    n = lax.axis_size(axis)
    return lax.ppermute(value, axis, [(i, (i + by) % n) for i in range(n)])


def on_device(features, weight, cotangent, tile_values, tile_rows, tile_cols, tile_count):
    own = features[0]
    per_dev, feat = own.shape
    slots = tile_values.shape[2]
    nz = lax.axis_size(Z)
    groups = 2 * nz
    n_chunks = groups // 3
    col_devs = lax.axis_size(COL)
    rows = per_dev * col_devs
    x = lax.axis_index("x")
    info = jnp.stack([x % 2, x // 2, lax.axis_index("yh"), lax.axis_index(COL), lax.axis_index("zb"), x]).astype(jnp.int32)
    params = pltpu.CompilerParams(vmem_limit_bytes=VMEM_LIMIT)
    vmem, smem = spec(pltpu.VMEM), spec(pltpu.SMEM)

    def call(kernel, name, ins, outs, scratch, *args):
        return pl.pallas_call(
            kernel,
            out_shape=tuple(jax.ShapeDtypeStruct(s, t) for s, t in outs),
            in_specs=ins,
            out_specs=(vmem,) * len(outs),
            scratch_shapes=scratch,
            compiler_params=params,
            name=name,
        )(*args)

    live = jnp.arange(slots, dtype=jnp.int32) < tile_count[0, 0]
    code = jnp.where(live, tile_rows[0, 0] + 4 * tile_cols[0, 0], -1)
    meta = jnp.pad(code.astype(F32), (0, TILE - slots))[None]

    near = jnp.concatenate([own, shift(own, "yh", 1)], axis=0)
    column = lax.all_gather(near, Z, axis=0, tiled=True)

    parcel = ((slots + 3, STRIP, TILE), BF)
    same, other = call(
        pack_kernel, "pack", [smem, vmem, vmem, vmem], [parcel] * 2, [], info, tile_values[0, 0], cotangent[0], meta
    )
    strips = [same] + [shift(same if d == 2 else other, "x", d) for d in (1, 2, 3)]
    codes = jnp.stack([code] + [s[slots + 2, 0, :slots].astype(jnp.int32) for s in strips[1:]])
    cots = jnp.stack([jnp.concatenate([s[slots], s[slots + 1]], axis=1) for s in strips])
    cot_all = lax.all_gather(cots.reshape(4 * STRIP, feat), COL, axis=0, tiled=True)
    cot_all = cot_all.reshape(col_devs, 4, STRIP, feat)

    listing = [pltpu.SMEM((3, 4 * slots + STEP), jnp.int32), pltpu.VMEM((4 * slots + 1, STRIP, TILE), BF)]
    parts = call(
        functools.partial(fwd_kernel, nz),
        "forward_tiles",
        [smem, smem] + [vmem] * 5,
        [((rows, feat), F32)] + [((rows, feat), BF)] * 3,
        listing + [pltpu.VMEM((16 * TILE, feat), F32)],
        codes, info, *strips, column,
    )

    back = [shift(parts[d], "x", -d) for d in (1, 2, 3)]
    block_sum = (parts[0] + (back[0].astype(F32) + back[1].astype(F32) + back[2].astype(F32))).astype(BF)
    pieces = lax.all_to_all(block_sum, COL, split_axis=0, concat_axis=0, tiled=True)
    agg = jnp.sum(pieces.reshape(col_devs, per_dev, feat).astype(F32), axis=0).astype(BF)
    block_agg = lax.all_gather(agg, COL, axis=0, tiled=True)
    aggs = [block_agg] + [shift(block_agg, "x", d) for d in (1, 2, 3)]

    share = feat // col_devs
    chunk_rows = n_chunks * STRIP
    output_rows, keep, up, down = call(
        functools.partial(bwd_kernel, nz),
        "backward_tiles",
        [smem, smem] + [vmem] * 10,
        [((per_dev, feat), BF), ((chunk_rows + share, feat), F32)] + [((chunk_rows + 2 * share, feat), BF)] * 2,
        listing
        + [
            pltpu.VMEM((16 * TILE, feat), BF),
            pltpu.VMEM((groups * STRIP, feat), F32),
            pltpu.VMEM((4, feat, feat), F32),
            pltpu.VMEM((rows, feat), F32),
        ],
        codes, info, *strips, *aggs, cot_all, weight,
    )
    (chunks,) = call(
        near_kernel,
        "near_sum",
        [vmem] * 3,
        [((n_chunks, STRIP + 2 * share, feat), BF)],
        [],
        keep, shift(up, Z, 1), shift(down, Z, -1),
    )
    arrived = lax.all_to_all(chunks, ("yh", "za"), split_axis=0, concat_axis=0, tiled=True)
    node_total = per_dev * lax.axis_size(ROW) * col_devs
    grads, weight_part = call(
        functools.partial(far_kernel, node_total ** (-0.5)),
        "far_sum",
        [vmem],
        [((per_dev, feat), BF), ((share, feat), F32)],
        [],
        arrived,
    )
    grad_weight = lax.all_gather(weight_part, COL, axis=0, tiled=True)
    return output_rows[None], grads[None], grad_weight


def build(mesh, split):
    grid = Mesh(mesh.devices.reshape(split), NAMES)
    return jax.shard_map(
        on_device,
        mesh=grid,
        in_specs=(
            P(COL, ROW, None),
            P(),
            P(ROW, COL, None),
            P(ROW, COL, None, None, None),
            P(ROW, COL, None),
            P(ROW, COL, None),
            P(ROW, COL),
        ),
        out_specs=(P(ROW, COL, None), P(COL, ROW, None), P()),
        check_vma=False,
    )


def solution(mesh):
    return build(mesh, SPLIT)
```

```python
import functools

import jax
import jax.numpy as jnp
from jax import lax
from jax.experimental import pallas as pl
from jax.experimental.pallas import tpu as pltpu
from jax.sharding import Mesh
from jax.sharding import PartitionSpec as P

BF = jnp.bfloat16
F32 = jnp.float32
TILE = 128
STRIP = 64
SPLIT = (2, 4, 3, 4, 4, 2)
NAMES = ("yh", "za", "zb", "x", "yl", "core")
ROW = ("yh", "za", "zb", "x")
Z = ("za", "zb")
STEP = 4
COL = ("yl", "core")
VMEM_LIMIT = 40 * 1024 * 1024


def spec(space):
    return pl.BlockSpec(memory_space=space)


def pack_kernel(info, tiles, meta, same, other):
    slots = tiles.shape[0]
    odd = info[0] == 1

    def one(s, carry):
        turned = tiles[s].T
        low, high = turned[:STRIP], turned[STRIP:]
        same[s] = jnp.where(odd, high, low)
        other[s] = jnp.where(odd, low, high)
        return carry

    lax.fori_loop(0, slots, one, 0, unroll=4)
    for ref in (same, other):
        ref[slots] = jnp.broadcast_to(meta[...], (STRIP, TILE)).astype(BF)


def live_list(codes, mine, row_of, place_of, table, strips, pool):
    slots = codes.shape[1]
    for j, ref in enumerate(strips):
        pool[j * slots : (j + 1) * slots] = ref[:slots]
    pool[4 * slots] = jnp.zeros((STRIP, TILE), BF)
    count = jnp.int32(0)
    for j in range(4):

        def one(s, n, j=j):
            code = codes[j, s]
            col, row = code >> 2, code & 3
            table[0, n] = j * slots + s
            table[1, n] = j * 4 + row_of(row)
            table[2, n] = place_of(col >> 1)
            return n + ((code >= 0) & ((col & 1) == mine)).astype(jnp.int32)

        count = lax.fori_loop(0, slots, one, count, unroll=4)
    for i in range(STEP):
        table[0, count + i] = 4 * slots
        table[1, count + i] = 0
        table[2, count + i] = 0
    return count


def fwd_kernel(nz, codes, info, s0, s1, s2, s3, feats, o0, o1, o2, o3, table, pool, acc):
    rows = o0.shape[0]
    mine, my_yh = info[1], info[2]

    def place_of(q):
        far = (q >= nz).astype(jnp.int32)
        return (q - far * nz) * 2 + (far ^ my_yh)

    count = live_list(codes, mine, lambda r: r, place_of, table, (s0, s1, s2, s3), pool)
    acc[...] = jnp.zeros_like(acc)

    def several(t, carry):
        terms = []
        for i in range(STEP):
            at = t * STEP + i
            block = feats[pl.ds(pl.multiple_of(table[2, at] * STRIP, STRIP), STRIP), :]
            term = lax.dot_general(
                pool[table[0, at]], block, (((0,), (0,)), ((), ())), preferred_element_type=F32
            )
            terms.append((pl.ds(pl.multiple_of(table[1, at] * TILE, TILE), TILE), term))
        for at, term in terms:
            acc[at, :] = acc[at, :] + term
        return carry

    lax.fori_loop(0, (count + (STEP - 1)) // STEP, several, 0)
    per = 4 * TILE
    for j, ref in enumerate((o0, o1, o2, o3)):
        ref[...] = acc[j * per : j * per + rows, :].astype(ref.dtype)


def bwd_kernel(
    nz, codes, info, s0, s1, s2, s3, a_own, a_other, c0, c1, c2, c3, w, out, keep, up, down,
    table, pool, agg, ga, acc, gw4, act,
):
    rows, feat = c0.shape
    mine, col_pos, my_zb, my_x = info[1], info[3], info[4], info[5]
    my_yl, my_core = col_pos >> 1, col_pos & 1
    share = keep.shape[0] - (acc.shape[0] // 3)
    n_yl = rows // TILE
    count = live_list(codes, mine, lambda r: (my_yl - r) & (n_yl - 1), lambda q: q, table, (s0, s1, s2, s3), pool)
    acc[...] = jnp.zeros_like(acc)
    per = 4 * TILE
    for j, cot in enumerate((c0, c1, c2, c3)):
        for d in range(n_yl):
            src = pl.ds(pl.multiple_of((((my_yl - d) & (n_yl - 1)) * 4 + j) * STRIP, STRIP), STRIP)
            for i, ref in enumerate((a_own, a_other)):
                to = pl.multiple_of(j * per + d * TILE + (my_core ^ i) * STRIP, STRIP)
                agg[pl.ds(to, STRIP), :] = ref[src, :]
        block = agg[j * per : j * per + rows, :]
        pre = jnp.dot(block, w[...], preferred_element_type=F32)
        sig = jax.nn.sigmoid(pre)
        if j == 0:
            act[...] = (pre * sig)[:TILE]
        slope = sig * (1.0 + pre * (1.0 - sig))
        gp = (cot[...].astype(F32) * slope).astype(BF)
        gw4[(my_x - j) & 3] = lax.dot_general(block, gp, (((0,), (0,)), ((), ())), preferred_element_type=F32)
        ga[j * per : j * per + rows, :] = lax.dot_general(
            gp, w[...], (((1,), (1,)), ((), ())), preferred_element_type=F32
        ).astype(BF)
    out[...] = act[pl.ds(pl.multiple_of(my_core * STRIP, STRIP), STRIP), :].astype(BF)

    def several(t, carry):
        terms = []
        for i in range(STEP):
            at = t * STEP + i
            block = ga[pl.ds(pl.multiple_of(table[1, at] * TILE, TILE), TILE), :]
            term = jnp.dot(pool[table[0, at]], block, preferred_element_type=F32)
            terms.append((pl.ds(pl.multiple_of(table[2, at] * STRIP, STRIP), STRIP), term))
        for at, term in terms:
            acc[at, :] = acc[at, :] + term
        return carry

    lax.fori_loop(0, (count + (STEP - 1)) // STEP, several, 0)
    mine_rows = pl.ds(pl.multiple_of(col_pos * share, share), share)
    part = (gw4[0, mine_rows, :] + gw4[1, mine_rows, :]) + (gw4[2, mine_rows, :] + gw4[3, mine_rows, :])
    high = part.astype(BF)
    low = (part - high.astype(F32)).astype(BF)
    n_chunks = acc.shape[0] // (3 * STRIP)
    n_za = nz // 3
    for base, ref in ((0, keep), (1, up), (2, down)):
        which = lax.rem(my_zb + base, 3)
        for i in range(n_chunks):
            q = (i // n_za) * nz + 3 * (i % n_za) + which
            block = acc[pl.ds(pl.multiple_of(q * STRIP, STRIP), STRIP), :]
            ref[i * STRIP : (i + 1) * STRIP, :] = block.astype(ref.dtype)
    end = n_chunks * STRIP
    keep[end:, :] = part
    for ref in (up, down):
        ref[end : end + share, :] = high
        ref[end + share :, :] = low


def near_kernel(keep, up, down, chunks):
    n_chunks = chunks.shape[0]
    end = n_chunks * STRIP
    share = keep.shape[0] - end
    for i in range(n_chunks):
        at = slice(i * STRIP, (i + 1) * STRIP)
        chunks[i, :STRIP, :] = (keep[at, :] + (up[at, :].astype(F32) + down[at, :].astype(F32))).astype(BF)
    part = keep[end:, :]
    for ref in (up, down):
        part = part + (ref[end : end + share, :].astype(F32) + ref[end + share :, :].astype(F32))
    high = part.astype(BF)
    low = (part - high.astype(F32)).astype(BF)
    for i in range(n_chunks):
        chunks[i, STRIP : STRIP + share, :] = high
        chunks[i, STRIP + share :, :] = low


def far_kernel(scale, chunks, grads, weight_part):
    share = weight_part.shape[0]
    total = jnp.sum(chunks[...].astype(F32), axis=0)
    grads[...] = total[:STRIP].astype(BF)
    weight_part[...] = (total[STRIP : STRIP + share] + total[STRIP + share :]) * scale


def shift(value, axis, by):
    n = lax.axis_size(axis)
    return lax.ppermute(value, axis, [(i, (i + by) % n) for i in range(n)])


def on_device(features, weight, cotangent, tile_values, tile_rows, tile_cols, tile_count):
    own = features[0]
    per_dev, feat = own.shape
    slots = tile_values.shape[2]
    nz = lax.axis_size(Z)
    groups = 2 * nz
    n_chunks = groups // 3
    col_devs = lax.axis_size(COL)
    rows = per_dev * col_devs
    x = lax.axis_index("x")
    info = jnp.stack([x % 2, x // 2, lax.axis_index("yh"), lax.axis_index(COL), lax.axis_index("zb"), x]).astype(jnp.int32)
    params = pltpu.CompilerParams(vmem_limit_bytes=VMEM_LIMIT)
    vmem, smem = spec(pltpu.VMEM), spec(pltpu.SMEM)

    def call(kernel, name, ins, outs, scratch, *args):
        return pl.pallas_call(
            kernel,
            out_shape=tuple(jax.ShapeDtypeStruct(s, t) for s, t in outs),
            in_specs=ins,
            out_specs=(vmem,) * len(outs),
            scratch_shapes=scratch,
            compiler_params=params,
            name=name,
        )(*args)

    live = jnp.arange(slots, dtype=jnp.int32) < tile_count[0, 0]
    code = jnp.where(live, tile_rows[0, 0] + 4 * tile_cols[0, 0], -1)
    meta = jnp.pad(code.astype(F32), (0, TILE - slots))[None]

    near = jnp.concatenate([own, shift(own, "yh", 1)], axis=0)

    parcel = ((slots + 1, STRIP, TILE), BF)
    same, other = call(pack_kernel, "pack", [smem, vmem, vmem], [parcel] * 2, [], info, tile_values[0, 0], meta)
    strips = [same] + [shift(same if d == 2 else other, "x", d) for d in (1, 2, 3)]
    codes = jnp.stack([code] + [s[slots, 0, :slots].astype(jnp.int32) for s in strips[1:]])

    pair = lax.all_gather(cotangent[0], "core", axis=0, tiled=True)
    n_yl = lax.axis_size("yl")
    pairs = [pair] + [shift(pair, "yl", d) for d in range(1, n_yl)]
    near, *pairs = lax.optimization_barrier((near, *pairs))
    block_cot = jnp.concatenate(pairs, axis=0)

    column = lax.all_gather(near, Z, axis=0, tiled=True)
    column, block_cot = lax.optimization_barrier((column, block_cot))

    listing = [pltpu.SMEM((3, 4 * slots + STEP), jnp.int32), pltpu.VMEM((4 * slots + 1, STRIP, TILE), BF)]
    parts = call(
        functools.partial(fwd_kernel, nz),
        "forward_tiles",
        [smem, smem] + [vmem] * 5,
        [((rows, feat), F32)] + [((rows, feat), BF)] * 3,
        listing + [pltpu.VMEM((16 * TILE, feat), F32)],
        codes, info, *strips, column,
    )

    back = [shift(parts[d], "x", -d) for d in (1, 2, 3)]
    block_sum = (parts[0] + (back[0].astype(F32) + back[1].astype(F32) + back[2].astype(F32))).astype(BF)
    pieces = lax.all_to_all(block_sum, COL, split_axis=0, concat_axis=0, tiled=True)
    cots = [block_cot] + [shift(block_cot, "x", d) for d in (1, 2, 3)]
    pieces, *cots = lax.optimization_barrier((pieces, *cots))
    agg = jnp.sum(pieces.reshape(col_devs, per_dev, feat).astype(F32), axis=0).astype(BF)
    group_agg = jnp.concatenate([agg] + [shift(agg, "x", d) for d in (1, 2, 3)], axis=0)
    core_agg = lax.all_gather(group_agg, "yl", axis=0, tiled=True)
    other_agg = shift(core_agg, "core", 1)

    share = feat // col_devs
    chunk_rows = n_chunks * STRIP
    output_rows, keep, up, down = call(
        functools.partial(bwd_kernel, nz),
        "backward_tiles",
        [smem, smem] + [vmem] * 11,
        [((per_dev, feat), BF), ((chunk_rows + share, feat), F32)] + [((chunk_rows + 2 * share, feat), BF)] * 2,
        listing
        + [
            pltpu.VMEM((16 * TILE, feat), BF),
            pltpu.VMEM((16 * TILE, feat), BF),
            pltpu.VMEM((groups * STRIP, feat), F32),
            pltpu.VMEM((4, feat, feat), F32),
            pltpu.VMEM((TILE, feat), F32),
        ],
        codes, info, *strips, core_agg, other_agg, *cots, weight,
    )
    (chunks,) = call(
        near_kernel,
        "near_sum",
        [vmem] * 3,
        [((n_chunks, STRIP + 2 * share, feat), BF)],
        [],
        keep, shift(up, Z, 1), shift(down, Z, -1),
    )
    arrived = lax.all_to_all(chunks, ("yh", "za"), split_axis=0, concat_axis=0, tiled=True)
    node_total = per_dev * lax.axis_size(ROW) * col_devs
    grads, weight_part = call(
        functools.partial(far_kernel, node_total ** (-0.5)),
        "far_sum",
        [vmem],
        [((per_dev, feat), BF), ((share, feat), F32)],
        [],
        arrived,
    )
    grad_weight = lax.all_gather(weight_part, COL, axis=0, tiled=True)
    return output_rows[None], grads[None], grad_weight


def build(mesh, split):
    grid = Mesh(mesh.devices.reshape(split), NAMES)
    return jax.shard_map(
        on_device,
        mesh=grid,
        in_specs=(
            P(COL, ROW, None),
            P(),
            P(ROW, COL, None),
            P(ROW, COL, None, None, None),
            P(ROW, COL, None),
            P(ROW, COL, None),
            P(ROW, COL),
        ),
        out_specs=(P(ROW, COL, None), P(COL, ROW, None), P()),
        check_vma=False,
    )


def solution(mesh):
    return build(mesh, SPLIT)
```

```python
import functools

import jax
import jax.numpy as jnp
from jax import lax
from jax.experimental import pallas as pl
from jax.experimental.pallas import tpu as pltpu
from jax.sharding import Mesh
from jax.sharding import PartitionSpec as P

BF = jnp.bfloat16
F32 = jnp.float32
TILE = 128
STRIP = 64
SPLIT = (2, 4, 3, 4, 4, 2)
NAMES = ("yh", "za", "zb", "x", "yl", "core")
ROW = ("yh", "za", "zb", "x")
Z = ("za", "zb")
STEP = 4
COL = ("yl", "core")
VMEM_LIMIT = 40 * 1024 * 1024


def spec(space):
    return pl.BlockSpec(memory_space=space)


def pack_kernel(info, tiles, meta, y0, y1, y2, y3, same, other):
    slots = tiles.shape[0]
    odd = info[0] == 1

    def one(s, carry):
        turned = tiles[s].T
        low, high = turned[:STRIP], turned[STRIP:]
        same[s] = jnp.where(odd, high, low)
        other[s] = jnp.where(odd, low, high)
        return carry

    lax.fori_loop(0, slots, one, 0, unroll=4)
    for ref in (same, other):
        ref[slots] = jnp.broadcast_to(meta[...], (STRIP, TILE)).astype(BF)
        for d, cot in enumerate((y0, y1, y2, y3)):
            ref[slots + 1 + 2 * d] = cot[:, :TILE]
            ref[slots + 2 + 2 * d] = cot[:, TILE:]


def live_list(codes, mine, row_of, place_of, table, strips, pool):
    slots = codes.shape[1]
    for j, ref in enumerate(strips):
        pool[j * slots : (j + 1) * slots] = ref[:slots]
    pool[4 * slots] = jnp.zeros((STRIP, TILE), BF)
    count = jnp.int32(0)
    for j in range(4):

        def one(s, n, j=j):
            code = codes[j, s]
            col, row = code >> 2, code & 3
            table[0, n] = j * slots + s
            table[1, n] = j * 4 + row_of(row)
            table[2, n] = place_of(col >> 1)
            return n + ((code >= 0) & ((col & 1) == mine)).astype(jnp.int32)

        count = lax.fori_loop(0, slots, one, count, unroll=4)
    for i in range(STEP):
        table[0, count + i] = 4 * slots
        table[1, count + i] = 0
        table[2, count + i] = 0
    return count


def fwd_kernel(nz, codes, info, s0, s1, s2, s3, feats, o0, o1, o2, o3, cots, table, pool, acc):
    rows = o0.shape[0]
    mine, my_yh = info[1], info[2]

    def place_of(q):
        far = (q >= nz).astype(jnp.int32)
        return (q - far * nz) * 2 + (far ^ my_yh)

    count = live_list(codes, mine, lambda r: r, place_of, table, (s0, s1, s2, s3), pool)
    acc[...] = jnp.zeros_like(acc)

    def several(t, carry):
        terms = []
        for i in range(STEP):
            at = t * STEP + i
            block = feats[pl.ds(pl.multiple_of(table[2, at] * STRIP, STRIP), STRIP), :]
            term = lax.dot_general(
                pool[table[0, at]], block, (((0,), (0,)), ((), ())), preferred_element_type=F32
            )
            terms.append((pl.ds(pl.multiple_of(table[1, at] * TILE, TILE), TILE), term))
        for at, term in terms:
            acc[at, :] = acc[at, :] + term
        return carry

    lax.fori_loop(0, (count + (STEP - 1)) // STEP, several, 0)
    per = 4 * TILE
    for j, ref in enumerate((o0, o1, o2, o3)):
        ref[...] = acc[j * per : j * per + rows, :].astype(ref.dtype)
    slots = codes.shape[1]
    for j, ref in enumerate((s0, s1, s2, s3)):
        for d in range(4):
            at = slice((4 * j + d) * STRIP, (4 * j + d + 1) * STRIP)
            cots[at, :TILE] = ref[slots + 1 + 2 * d]
            cots[at, TILE:] = ref[slots + 2 + 2 * d]


def bwd_kernel(
    nz, codes, info, s0, s1, s2, s3, a_own, a_other, c_own, c_other, w, out, keep, up, down,
    table, pool, agg, cots, ga, acc, gw4, act,
):
    rows, feat = 4 * TILE, w.shape[0]
    mine, col_pos, my_zb, my_x = info[1], info[3], info[4], info[5]
    my_yl, my_core = col_pos >> 1, col_pos & 1
    share = keep.shape[0] - (acc.shape[0] // 3)
    n_yl = rows // TILE
    count = live_list(codes, mine, lambda r: (my_yl - r) & (n_yl - 1), lambda q: q, table, (s0, s1, s2, s3), pool)
    acc[...] = jnp.zeros_like(acc)
    per = 4 * TILE
    for j in range(4):
        for d in range(n_yl):
            src = pl.ds(pl.multiple_of((((my_yl - d) & (n_yl - 1)) * 4 + j) * STRIP, STRIP), STRIP)
            here = slice((4 * j + d) * STRIP, (4 * j + d + 1) * STRIP)
            for i, (rows_in, cots_in) in enumerate(((a_own, c_own), (a_other, c_other))):
                to = pl.multiple_of(j * per + d * TILE + (my_core ^ i) * STRIP, STRIP)
                agg[pl.ds(to, STRIP), :] = rows_in[src, :]
                cots[pl.ds(to, STRIP), :] = cots_in[here, :]
        block = agg[j * per : j * per + rows, :]
        pre = jnp.dot(block, w[...], preferred_element_type=F32)
        sig = jax.nn.sigmoid(pre)
        if j == 0:
            act[...] = (pre * sig)[:TILE]
        slope = sig * (1.0 + pre * (1.0 - sig))
        gp = (cots[j * per : j * per + rows, :].astype(F32) * slope).astype(BF)
        gw4[(my_x - j) & 3] = lax.dot_general(block, gp, (((0,), (0,)), ((), ())), preferred_element_type=F32)
        ga[j * per : j * per + rows, :] = lax.dot_general(
            gp, w[...], (((1,), (1,)), ((), ())), preferred_element_type=F32
        ).astype(BF)
    out[...] = act[pl.ds(pl.multiple_of(my_core * STRIP, STRIP), STRIP), :].astype(BF)

    def several(t, carry):
        terms = []
        for i in range(STEP):
            at = t * STEP + i
            block = ga[pl.ds(pl.multiple_of(table[1, at] * TILE, TILE), TILE), :]
            term = jnp.dot(pool[table[0, at]], block, preferred_element_type=F32)
            terms.append((pl.ds(pl.multiple_of(table[2, at] * STRIP, STRIP), STRIP), term))
        for at, term in terms:
            acc[at, :] = acc[at, :] + term
        return carry

    lax.fori_loop(0, (count + (STEP - 1)) // STEP, several, 0)
    mine_rows = pl.ds(pl.multiple_of(col_pos * share, share), share)
    part = (gw4[0, mine_rows, :] + gw4[1, mine_rows, :]) + (gw4[2, mine_rows, :] + gw4[3, mine_rows, :])
    high = part.astype(BF)
    low = (part - high.astype(F32)).astype(BF)
    n_chunks = acc.shape[0] // (3 * STRIP)
    n_za = nz // 3
    for base, ref in ((0, keep), (1, up), (2, down)):
        which = lax.rem(my_zb + base, 3)
        for i in range(n_chunks):
            q = (i // n_za) * nz + 3 * (i % n_za) + which
            block = acc[pl.ds(pl.multiple_of(q * STRIP, STRIP), STRIP), :]
            ref[i * STRIP : (i + 1) * STRIP, :] = block.astype(ref.dtype)
    end = n_chunks * STRIP
    keep[end:, :] = part
    for ref in (up, down):
        ref[end : end + share, :] = high
        ref[end + share :, :] = low


def near_kernel(keep, up, down, chunks):
    n_chunks = chunks.shape[0]
    end = n_chunks * STRIP
    share = keep.shape[0] - end
    for i in range(n_chunks):
        at = slice(i * STRIP, (i + 1) * STRIP)
        chunks[i, :STRIP, :] = (keep[at, :] + (up[at, :].astype(F32) + down[at, :].astype(F32))).astype(BF)
    part = keep[end:, :]
    for ref in (up, down):
        part = part + (ref[end : end + share, :].astype(F32) + ref[end + share :, :].astype(F32))
    high = part.astype(BF)
    low = (part - high.astype(F32)).astype(BF)
    for i in range(n_chunks):
        chunks[i, STRIP : STRIP + share, :] = high
        chunks[i, STRIP + share :, :] = low


def far_kernel(scale, chunks, grads, weight_part):
    share = weight_part.shape[0]
    total = jnp.sum(chunks[...].astype(F32), axis=0)
    grads[...] = total[:STRIP].astype(BF)
    weight_part[...] = (total[STRIP : STRIP + share] + total[STRIP + share :]) * scale


def shift(value, axis, by):
    n = lax.axis_size(axis)
    return lax.ppermute(value, axis, [(i, (i + by) % n) for i in range(n)])


def on_device(features, weight, cotangent, tile_values, tile_rows, tile_cols, tile_count):
    own = features[0]
    per_dev, feat = own.shape
    slots = tile_values.shape[2]
    nz = lax.axis_size(Z)
    groups = 2 * nz
    n_chunks = groups // 3
    col_devs = lax.axis_size(COL)
    rows = per_dev * col_devs
    x = lax.axis_index("x")
    info = jnp.stack([x % 2, x // 2, lax.axis_index("yh"), lax.axis_index(COL), lax.axis_index("zb"), x]).astype(jnp.int32)
    params = pltpu.CompilerParams(vmem_limit_bytes=VMEM_LIMIT)
    vmem, smem = spec(pltpu.VMEM), spec(pltpu.SMEM)

    def call(kernel, name, ins, outs, scratch, *args):
        return pl.pallas_call(
            kernel,
            out_shape=tuple(jax.ShapeDtypeStruct(s, t) for s, t in outs),
            in_specs=ins,
            out_specs=(vmem,) * len(outs),
            scratch_shapes=scratch,
            compiler_params=params,
            name=name,
        )(*args)

    live = jnp.arange(slots, dtype=jnp.int32) < tile_count[0, 0]
    code = jnp.where(live, tile_rows[0, 0] + 4 * tile_cols[0, 0], -1)
    meta = jnp.pad(code.astype(F32), (0, TILE - slots))[None]

    near = jnp.concatenate([own, shift(own, "yh", 1)], axis=0)

    n_yl = lax.axis_size("yl")
    cots = [cotangent[0]] + [shift(cotangent[0], "yl", d) for d in range(1, n_yl)]

    parcel = ((slots + 1 + 2 * n_yl, STRIP, TILE), BF)
    same, other = call(
        pack_kernel, "pack", [smem] + [vmem] * 6, [parcel] * 2, [], info, tile_values[0, 0], meta, *cots
    )
    strips = [same] + [shift(same if d == 2 else other, "x", d) for d in (1, 2, 3)]
    codes = jnp.stack([code] + [s[slots, 0, :slots].astype(jnp.int32) for s in strips[1:]])
    column = lax.all_gather(near, Z, axis=0, tiled=True)

    listing = [pltpu.SMEM((3, 4 * slots + STEP), jnp.int32), pltpu.VMEM((4 * slots + 1, STRIP, TILE), BF)]
    *parts, core_cots = call(
        functools.partial(fwd_kernel, nz),
        "forward_tiles",
        [smem, smem] + [vmem] * 5,
        [((rows, feat), F32)] + [((rows, feat), BF)] * 3 + [((4 * n_yl * STRIP, feat), BF)],
        listing + [pltpu.VMEM((16 * TILE, feat), F32)],
        codes, info, *strips, column,
    )

    back = [shift(parts[d], "x", -d) for d in (1, 2, 3)]
    block_sum = (parts[0] + (back[0].astype(F32) + back[1].astype(F32) + back[2].astype(F32))).astype(BF)
    other_cots = shift(core_cots, "core", 1)
    block_sum, other_cots = lax.optimization_barrier((block_sum, other_cots))
    pieces = lax.all_to_all(block_sum, COL, split_axis=0, concat_axis=0, tiled=True)
    agg = jnp.sum(pieces.reshape(col_devs, per_dev, feat).astype(F32), axis=0).astype(BF)
    group_agg = jnp.concatenate([agg] + [shift(agg, "x", d) for d in (1, 2, 3)], axis=0)
    core_agg = lax.all_gather(group_agg, "yl", axis=0, tiled=True)
    other_agg = shift(core_agg, "core", 1)

    share = feat // col_devs
    chunk_rows = n_chunks * STRIP
    output_rows, keep, up, down = call(
        functools.partial(bwd_kernel, nz),
        "backward_tiles",
        [smem, smem] + [vmem] * 9,
        [((per_dev, feat), BF), ((chunk_rows + share, feat), F32)] + [((chunk_rows + 2 * share, feat), BF)] * 2,
        listing
        + [
            pltpu.VMEM((16 * TILE, feat), BF),
            pltpu.VMEM((16 * TILE, feat), BF),
            pltpu.VMEM((16 * TILE, feat), BF),
            pltpu.VMEM((groups * STRIP, feat), F32),
            pltpu.VMEM((4, feat, feat), F32),
            pltpu.VMEM((TILE, feat), F32),
        ],
        codes, info, *strips, core_agg, other_agg, core_cots, other_cots, weight,
    )
    (chunks,) = call(
        near_kernel,
        "near_sum",
        [vmem] * 3,
        [((n_chunks, STRIP + 2 * share, feat), BF)],
        [],
        keep, shift(up, Z, 1), shift(down, Z, -1),
    )
    arrived = lax.all_to_all(chunks, ("yh", "za"), split_axis=0, concat_axis=0, tiled=True)
    node_total = per_dev * lax.axis_size(ROW) * col_devs
    grads, weight_part = call(
        functools.partial(far_kernel, node_total ** (-0.5)),
        "far_sum",
        [vmem],
        [((per_dev, feat), BF), ((share, feat), F32)],
        [],
        arrived,
    )
    grad_weight = lax.all_gather(weight_part, COL, axis=0, tiled=True)
    return output_rows[None], grads[None], grad_weight


def build(mesh, split):
    grid = Mesh(mesh.devices.reshape(split), NAMES)
    return jax.shard_map(
        on_device,
        mesh=grid,
        in_specs=(
            P(COL, ROW, None),
            P(),
            P(ROW, COL, None),
            P(ROW, COL, None, None, None),
            P(ROW, COL, None),
            P(ROW, COL, None),
            P(ROW, COL),
        ),
        out_specs=(P(ROW, COL, None), P(COL, ROW, None), P()),
        check_vma=False,
    )


def solution(mesh):
    return build(mesh, SPLIT)
```

```python
import functools

import jax
import jax.numpy as jnp
from jax import lax
from jax.experimental import pallas as pl
from jax.experimental.pallas import tpu as pltpu
from jax.sharding import Mesh
from jax.sharding import PartitionSpec as P

BF = jnp.bfloat16
F32 = jnp.float32
TILE = 128
STRIP = 64
SPLIT = (2, 4, 3, 4, 4, 2)
NAMES = ("yh", "za", "zb", "x", "yl", "core")
ROW = ("yh", "za", "zb", "x")
Z = ("za", "zb")
STEP = 4
COL = ("yl", "core")
VMEM_LIMIT = 40 * 1024 * 1024


def spec(space):
    return pl.BlockSpec(memory_space=space)


def pack_kernel(info, tiles, meta, cot, same, other):
    slots = tiles.shape[0]
    odd = info[0] == 1

    def one(s, carry):
        turned = tiles[s].T
        low, high = turned[:STRIP], turned[STRIP:]
        same[s] = jnp.where(odd, high, low)
        other[s] = jnp.where(odd, low, high)
        return carry

    lax.fori_loop(0, slots, one, 0, unroll=4)
    for ref in (same, other):
        ref[slots] = jnp.broadcast_to(meta[...], (STRIP, TILE)).astype(BF)
        ref[slots + 1] = cot[:, :TILE]
        ref[slots + 2] = cot[:, TILE:]


def live_list(codes, mine, row_of, place_of, table, strips, pool):
    slots = codes.shape[1]
    for j, ref in enumerate(strips):
        pool[j * slots : (j + 1) * slots] = ref[:slots]
    pool[4 * slots] = jnp.zeros((STRIP, TILE), BF)
    count = jnp.int32(0)
    for j in range(4):

        def one(s, n, j=j):
            code = codes[j, s]
            col, row = code >> 2, code & 3
            table[0, n] = j * slots + s
            table[1, n] = j * 4 + row_of(row)
            table[2, n] = place_of(col >> 1)
            return n + ((code >= 0) & ((col & 1) == mine)).astype(jnp.int32)

        count = lax.fori_loop(0, slots, one, count, unroll=4)
    for i in range(STEP):
        table[0, count + i] = 4 * slots
        table[1, count + i] = 0
        table[2, count + i] = 0
    return count


def fwd_kernel(nz, codes, info, s0, s1, s2, s3, feats, o0, o1, o2, o3, table, pool, acc):
    rows = o0.shape[0]
    mine, my_yh = info[1], info[2]

    def place_of(q):
        far = (q >= nz).astype(jnp.int32)
        return (q - far * nz) * 2 + (far ^ my_yh)

    count = live_list(codes, mine, lambda r: r, place_of, table, (s0, s1, s2, s3), pool)
    acc[...] = jnp.zeros_like(acc)

    def several(t, carry):
        terms = []
        for i in range(STEP):
            at = t * STEP + i
            block = feats[pl.ds(pl.multiple_of(table[2, at] * STRIP, STRIP), STRIP), :]
            term = lax.dot_general(
                pool[table[0, at]], block, (((0,), (0,)), ((), ())), preferred_element_type=F32
            )
            terms.append((pl.ds(pl.multiple_of(table[1, at] * TILE, TILE), TILE), term))
        for at, term in terms:
            acc[at, :] = acc[at, :] + term
        return carry

    lax.fori_loop(0, (count + (STEP - 1)) // STEP, several, 0)
    per = 4 * TILE
    for j, ref in enumerate((o0, o1, o2, o3)):
        ref[...] = acc[j * per : j * per + rows, :].astype(ref.dtype)


def bwd_kernel(
    nz, codes, info, s0, s1, s2, s3, a_own, a_other, c_own, c_other, w, out, keep, up, down,
    table, pool, agg, cots, ga, acc, gw4, act,
):
    rows, feat = 4 * TILE, w.shape[0]
    mine, col_pos, my_zb, my_x = info[1], info[3], info[4], info[5]
    my_yl, my_core = col_pos >> 1, col_pos & 1
    share = keep.shape[0] - (acc.shape[0] // 3)
    n_yl = rows // TILE
    count = live_list(codes, mine, lambda r: (my_yl - r) & (n_yl - 1), lambda q: q, table, (s0, s1, s2, s3), pool)
    acc[...] = jnp.zeros_like(acc)
    per = 4 * TILE
    for j in range(4):
        for d in range(n_yl):
            src = pl.ds(pl.multiple_of((((my_yl - d) & (n_yl - 1)) * 4 + j) * STRIP, STRIP), STRIP)
            for i, (rows_in, cots_in) in enumerate(((a_own, c_own), (a_other, c_other))):
                to = pl.multiple_of(j * per + d * TILE + (my_core ^ i) * STRIP, STRIP)
                agg[pl.ds(to, STRIP), :] = rows_in[src, :]
                cots[pl.ds(to, STRIP), :] = cots_in[src, :]
        block = agg[j * per : j * per + rows, :]
        pre = jnp.dot(block, w[...], preferred_element_type=F32)
        sig = jax.nn.sigmoid(pre)
        if j == 0:
            act[...] = (pre * sig)[:TILE]
        slope = sig * (1.0 + pre * (1.0 - sig))
        gp = (cots[j * per : j * per + rows, :].astype(F32) * slope).astype(BF)
        gw4[(my_x - j) & 3] = lax.dot_general(block, gp, (((0,), (0,)), ((), ())), preferred_element_type=F32)
        ga[j * per : j * per + rows, :] = lax.dot_general(
            gp, w[...], (((1,), (1,)), ((), ())), preferred_element_type=F32
        ).astype(BF)
    out[...] = act[pl.ds(pl.multiple_of(my_core * STRIP, STRIP), STRIP), :].astype(BF)

    def several(t, carry):
        terms = []
        for i in range(STEP):
            at = t * STEP + i
            block = ga[pl.ds(pl.multiple_of(table[1, at] * TILE, TILE), TILE), :]
            term = jnp.dot(pool[table[0, at]], block, preferred_element_type=F32)
            terms.append((pl.ds(pl.multiple_of(table[2, at] * STRIP, STRIP), STRIP), term))
        for at, term in terms:
            acc[at, :] = acc[at, :] + term
        return carry

    lax.fori_loop(0, (count + (STEP - 1)) // STEP, several, 0)
    mine_rows = pl.ds(pl.multiple_of(col_pos * share, share), share)
    part = (gw4[0, mine_rows, :] + gw4[1, mine_rows, :]) + (gw4[2, mine_rows, :] + gw4[3, mine_rows, :])
    high = part.astype(BF)
    low = (part - high.astype(F32)).astype(BF)
    n_chunks = acc.shape[0] // (3 * STRIP)
    n_za = nz // 3
    for base, ref in ((0, keep), (1, up), (2, down)):
        which = lax.rem(my_zb + base, 3)
        for i in range(n_chunks):
            q = (i // n_za) * nz + 3 * (i % n_za) + which
            block = acc[pl.ds(pl.multiple_of(q * STRIP, STRIP), STRIP), :]
            ref[i * STRIP : (i + 1) * STRIP, :] = block.astype(ref.dtype)
    end = n_chunks * STRIP
    keep[end:, :] = part
    for ref in (up, down):
        ref[end : end + share, :] = high
        ref[end + share :, :] = low


def near_kernel(keep, up, down, chunks):
    n_chunks = chunks.shape[0]
    end = n_chunks * STRIP
    share = keep.shape[0] - end
    for i in range(n_chunks):
        at = slice(i * STRIP, (i + 1) * STRIP)
        chunks[i, :STRIP, :] = (keep[at, :] + (up[at, :].astype(F32) + down[at, :].astype(F32))).astype(BF)
    part = keep[end:, :]
    for ref in (up, down):
        part = part + (ref[end : end + share, :].astype(F32) + ref[end + share :, :].astype(F32))
    high = part.astype(BF)
    low = (part - high.astype(F32)).astype(BF)
    for i in range(n_chunks):
        chunks[i, STRIP : STRIP + share, :] = high
        chunks[i, STRIP + share :, :] = low


def far_kernel(scale, chunks, grads, weight_part):
    share = weight_part.shape[0]
    total = jnp.sum(chunks[...].astype(F32), axis=0)
    grads[...] = total[:STRIP].astype(BF)
    weight_part[...] = (total[STRIP : STRIP + share] + total[STRIP + share :]) * scale


def shift(value, axis, by):
    n = lax.axis_size(axis)
    return lax.ppermute(value, axis, [(i, (i + by) % n) for i in range(n)])


def on_device(features, weight, cotangent, tile_values, tile_rows, tile_cols, tile_count):
    own = features[0]
    per_dev, feat = own.shape
    slots = tile_values.shape[2]
    nz = lax.axis_size(Z)
    groups = 2 * nz
    n_chunks = groups // 3
    col_devs = lax.axis_size(COL)
    rows = per_dev * col_devs
    x = lax.axis_index("x")
    info = jnp.stack([x % 2, x // 2, lax.axis_index("yh"), lax.axis_index(COL), lax.axis_index("zb"), x]).astype(jnp.int32)
    params = pltpu.CompilerParams(vmem_limit_bytes=VMEM_LIMIT)
    vmem, smem = spec(pltpu.VMEM), spec(pltpu.SMEM)

    def call(kernel, name, ins, outs, scratch, *args):
        return pl.pallas_call(
            kernel,
            out_shape=tuple(jax.ShapeDtypeStruct(s, t) for s, t in outs),
            in_specs=ins,
            out_specs=(vmem,) * len(outs),
            scratch_shapes=scratch,
            compiler_params=params,
            name=name,
        )(*args)

    live = jnp.arange(slots, dtype=jnp.int32) < tile_count[0, 0]
    code = jnp.where(live, tile_rows[0, 0] + 4 * tile_cols[0, 0], -1)
    meta = jnp.pad(code.astype(F32), (0, TILE - slots))[None]

    near = jnp.concatenate([own, shift(own, "yh", 1)], axis=0)

    parcel = ((slots + 3, STRIP, TILE), BF)
    same, other = call(
        pack_kernel, "pack", [smem] + [vmem] * 3, [parcel] * 2, [], info, tile_values[0, 0], meta, cotangent[0]
    )
    strips = [same] + [shift(same if d == 2 else other, "x", d) for d in (1, 2, 3)]
    codes = jnp.stack([code] + [s[slots, 0, :slots].astype(jnp.int32) for s in strips[1:]])
    cots = [jnp.concatenate([s[slots + 1], s[slots + 2]], axis=1) for s in strips]
    column = lax.all_gather(near, Z, axis=0, tiled=True)

    listing = [pltpu.SMEM((3, 4 * slots + STEP), jnp.int32), pltpu.VMEM((4 * slots + 1, STRIP, TILE), BF)]
    parts = call(
        functools.partial(fwd_kernel, nz),
        "forward_tiles",
        [smem, smem] + [vmem] * 5,
        [((rows, feat), F32)] + [((rows, feat), BF)] * 3,
        listing + [pltpu.VMEM((16 * TILE, feat), F32)],
        codes, info, *strips, column,
    )

    back = [shift(parts[d], "x", -d) for d in (1, 2, 3)]
    block_sum = (parts[0] + (back[0].astype(F32) + back[1].astype(F32) + back[2].astype(F32))).astype(BF)
    core_cots = lax.all_gather(jnp.concatenate(cots, axis=0), "yl", axis=0, tiled=True)
    block_sum, core_cots = lax.optimization_barrier((block_sum, core_cots))
    pieces = lax.all_to_all(block_sum, COL, split_axis=0, concat_axis=0, tiled=True)
    agg = jnp.sum(pieces.reshape(col_devs, per_dev, feat).astype(F32), axis=0).astype(BF)
    group_agg = jnp.concatenate([agg] + [shift(agg, "x", d) for d in (1, 2, 3)], axis=0)
    other_cots = shift(core_cots, "core", 1)
    group_agg, other_cots = lax.optimization_barrier((group_agg, other_cots))
    core_agg = lax.all_gather(group_agg, "yl", axis=0, tiled=True)
    other_agg = shift(core_agg, "core", 1)

    share = feat // col_devs
    chunk_rows = n_chunks * STRIP
    output_rows, keep, up, down = call(
        functools.partial(bwd_kernel, nz),
        "backward_tiles",
        [smem, smem] + [vmem] * 9,
        [((per_dev, feat), BF), ((chunk_rows + share, feat), F32)] + [((chunk_rows + 2 * share, feat), BF)] * 2,
        listing
        + [
            pltpu.VMEM((16 * TILE, feat), BF),
            pltpu.VMEM((16 * TILE, feat), BF),
            pltpu.VMEM((16 * TILE, feat), BF),
            pltpu.VMEM((groups * STRIP, feat), F32),
            pltpu.VMEM((4, feat, feat), F32),
            pltpu.VMEM((TILE, feat), F32),
        ],
        codes, info, *strips, core_agg, other_agg, core_cots, other_cots, weight,
    )
    (chunks,) = call(
        near_kernel,
        "near_sum",
        [vmem] * 3,
        [((n_chunks, STRIP + 2 * share, feat), BF)],
        [],
        keep, shift(up, Z, 1), shift(down, Z, -1),
    )
    arrived = lax.all_to_all(chunks, ("yh", "za"), split_axis=0, concat_axis=0, tiled=True)
    node_total = per_dev * lax.axis_size(ROW) * col_devs
    grads, weight_part = call(
        functools.partial(far_kernel, node_total ** (-0.5)),
        "far_sum",
        [vmem],
        [((per_dev, feat), BF), ((share, feat), F32)],
        [],
        arrived,
    )
    grad_weight = lax.all_gather(weight_part, COL, axis=0, tiled=True)
    return output_rows[None], grads[None], grad_weight


def build(mesh, split):
    grid = Mesh(mesh.devices.reshape(split), NAMES)
    return jax.shard_map(
        on_device,
        mesh=grid,
        in_specs=(
            P(COL, ROW, None),
            P(),
            P(ROW, COL, None),
            P(ROW, COL, None, None, None),
            P(ROW, COL, None),
            P(ROW, COL, None),
            P(ROW, COL),
        ),
        out_specs=(P(ROW, COL, None), P(COL, ROW, None), P()),
        check_vma=False,
    )


def solution(mesh):
    return build(mesh, SPLIT)
```

```python
import functools

import jax
import jax.numpy as jnp
from jax import lax
from jax.experimental import pallas as pl
from jax.experimental.pallas import tpu as pltpu
from jax.sharding import Mesh
from jax.sharding import PartitionSpec as P

BF = jnp.bfloat16
F32 = jnp.float32
TILE = 128
STRIP = 64
SPLIT = (2, 3, 4, 4, 4, 2)
NAMES = ("yh", "za", "zb", "x", "yl", "core")
ROW = ("yh", "za", "zb", "x")
Z = ("za", "zb")
STEP = 4
COL = ("yl", "core")
VMEM_LIMIT = 40 * 1024 * 1024


def spec(space):
    return pl.BlockSpec(memory_space=space)


def pack_kernel(info, tiles, meta, cot, same, other):
    slots = tiles.shape[0]
    odd = info[0] == 1

    def one(s, carry):
        turned = tiles[s].T
        low, high = turned[:STRIP], turned[STRIP:]
        same[s] = jnp.where(odd, high, low)
        other[s] = jnp.where(odd, low, high)
        return carry

    lax.fori_loop(0, slots, one, 0, unroll=4)
    for ref in (same, other):
        ref[slots] = jnp.broadcast_to(meta[...], (STRIP, TILE)).astype(BF)
        ref[slots + 1] = cot[:, :TILE]
        ref[slots + 2] = cot[:, TILE:]


def live_list(codes, mine, row_of, place_of, table, strips, pool):
    slots = codes.shape[1]
    for j, ref in enumerate(strips):
        pool[j * slots : (j + 1) * slots] = ref[:slots]
    pool[4 * slots] = jnp.zeros((STRIP, TILE), BF)
    count = jnp.int32(0)
    for j in range(4):

        def one(s, n, j=j):
            code = codes[j, s]
            col, row = code >> 2, code & 3
            table[0, n] = j * slots + s
            table[1, n] = j * 4 + row_of(row)
            table[2, n] = place_of(col >> 1)
            return n + ((code >= 0) & ((col & 1) == mine)).astype(jnp.int32)

        count = lax.fori_loop(0, slots, one, count, unroll=4)
    for i in range(STEP):
        table[0, count + i] = 4 * slots
        table[1, count + i] = 0
        table[2, count + i] = 0
    return count


def fwd_kernel(nz, codes, info, s0, s1, s2, s3, feats, o0, o1, o2, o3, table, pool, acc):
    rows = o0.shape[0]
    mine, my_yh = info[1], info[2]

    def place_of(q):
        far = (q >= nz).astype(jnp.int32)
        return (q - far * nz) * 2 + (far ^ my_yh)

    count = live_list(codes, mine, lambda r: r, place_of, table, (s0, s1, s2, s3), pool)
    acc[...] = jnp.zeros_like(acc)

    def several(t, carry):
        terms = []
        for i in range(STEP):
            at = t * STEP + i
            block = feats[pl.ds(pl.multiple_of(table[2, at] * STRIP, STRIP), STRIP), :]
            term = lax.dot_general(
                pool[table[0, at]], block, (((0,), (0,)), ((), ())), preferred_element_type=F32
            )
            terms.append((pl.ds(pl.multiple_of(table[1, at] * TILE, TILE), TILE), term))
        for at, term in terms:
            acc[at, :] = acc[at, :] + term
        return carry

    lax.fori_loop(0, (count + (STEP - 1)) // STEP, several, 0)
    per = 4 * TILE
    for j, ref in enumerate((o0, o1, o2, o3)):
        ref[...] = acc[j * per : j * per + rows, :].astype(ref.dtype)


def bwd_kernel(
    nz, codes, info, s0, s1, s2, s3, a_own, a_other, c_own, c_other, w, out, keep, up, down, back,
    table, pool, agg, cots, ga, acc, gw4, act,
):
    rows, feat = 4 * TILE, w.shape[0]
    mine, col_pos, my_zb, my_x = info[1], info[3], info[4], info[5]
    my_yl, my_core = col_pos >> 1, col_pos & 1
    share = keep.shape[0] - (acc.shape[0] // 4)
    n_yl = rows // TILE
    count = live_list(codes, mine, lambda r: (my_yl - r) & (n_yl - 1), lambda q: q, table, (s0, s1, s2, s3), pool)
    acc[...] = jnp.zeros_like(acc)
    per = 4 * TILE
    for j in range(4):
        for d in range(n_yl):
            src = pl.ds(pl.multiple_of((((my_yl - d) & (n_yl - 1)) * 4 + j) * STRIP, STRIP), STRIP)
            for i, (rows_in, cots_in) in enumerate(((a_own, c_own), (a_other, c_other))):
                to = pl.multiple_of(j * per + d * TILE + (my_core ^ i) * STRIP, STRIP)
                agg[pl.ds(to, STRIP), :] = rows_in[src, :]
                cots[pl.ds(to, STRIP), :] = cots_in[src, :]
        block = agg[j * per : j * per + rows, :]
        pre = jnp.dot(block, w[...], preferred_element_type=F32)
        sig = jax.nn.sigmoid(pre)
        if j == 0:
            act[...] = (pre * sig)[:TILE]
        slope = sig * (1.0 + pre * (1.0 - sig))
        gp = (cots[j * per : j * per + rows, :].astype(F32) * slope).astype(BF)
        gw4[(my_x - j) & 3] = lax.dot_general(block, gp, (((0,), (0,)), ((), ())), preferred_element_type=F32)
        ga[j * per : j * per + rows, :] = lax.dot_general(
            gp, w[...], (((1,), (1,)), ((), ())), preferred_element_type=F32
        ).astype(BF)
    out[...] = act[pl.ds(pl.multiple_of(my_core * STRIP, STRIP), STRIP), :].astype(BF)

    def several(t, carry):
        terms = []
        for i in range(STEP):
            at = t * STEP + i
            block = ga[pl.ds(pl.multiple_of(table[1, at] * TILE, TILE), TILE), :]
            term = jnp.dot(pool[table[0, at]], block, preferred_element_type=F32)
            terms.append((pl.ds(pl.multiple_of(table[2, at] * STRIP, STRIP), STRIP), term))
        for at, term in terms:
            acc[at, :] = acc[at, :] + term
        return carry

    lax.fori_loop(0, (count + (STEP - 1)) // STEP, several, 0)
    mine_rows = pl.ds(pl.multiple_of(col_pos * share, share), share)
    part = (gw4[0, mine_rows, :] + gw4[1, mine_rows, :]) + (gw4[2, mine_rows, :] + gw4[3, mine_rows, :])
    high = part.astype(BF)
    low = (part - high.astype(F32)).astype(BF)
    n_chunks = acc.shape[0] // (4 * STRIP)
    n_za = nz // 4
    for base, ref in ((0, keep), (1, up), (3, down), (2, back)):
        which = (my_zb + base) & 3
        for i in range(n_chunks):
            q = (i // n_za) * nz + 4 * (i % n_za) + which
            block = acc[pl.ds(pl.multiple_of(q * STRIP, STRIP), STRIP), :]
            ref[i * STRIP : (i + 1) * STRIP, :] = block.astype(ref.dtype)
    end = n_chunks * STRIP
    keep[end:, :] = part
    for ref in (up, down, back):
        ref[end : end + share, :] = high
        ref[end + share :, :] = low


def near_kernel(keep, up, down, back, chunks):
    n_chunks = chunks.shape[0]
    end = n_chunks * STRIP
    share = keep.shape[0] - end
    for i in range(n_chunks):
        at = slice(i * STRIP, (i + 1) * STRIP)
        chunks[i, :STRIP, :] = (
            (keep[at, :] + up[at, :].astype(F32)) + (down[at, :].astype(F32) + back[at, :].astype(F32))
        ).astype(BF)
    part = keep[end:, :]
    for ref in (up, down, back):
        part = part + (ref[end : end + share, :].astype(F32) + ref[end + share :, :].astype(F32))
    high = part.astype(BF)
    low = (part - high.astype(F32)).astype(BF)
    for i in range(n_chunks):
        chunks[i, STRIP : STRIP + share, :] = high
        chunks[i, STRIP + share :, :] = low


def far_kernel(scale, chunks, grads, weight_part):
    share = weight_part.shape[0]
    total = jnp.sum(chunks[...].astype(F32), axis=0)
    grads[...] = total[:STRIP].astype(BF)
    weight_part[...] = (total[STRIP : STRIP + share] + total[STRIP + share :]) * scale


def shift(value, axis, by):
    n = lax.axis_size(axis)
    return lax.ppermute(value, axis, [(i, (i + by) % n) for i in range(n)])


def on_device(features, weight, cotangent, tile_values, tile_rows, tile_cols, tile_count):
    own = features[0]
    per_dev, feat = own.shape
    slots = tile_values.shape[2]
    nz = lax.axis_size(Z)
    groups = 2 * nz
    n_chunks = groups // 4
    col_devs = lax.axis_size(COL)
    rows = per_dev * col_devs
    x = lax.axis_index("x")
    info = jnp.stack([x % 2, x // 2, lax.axis_index("yh"), lax.axis_index(COL), lax.axis_index("zb"), x]).astype(jnp.int32)
    params = pltpu.CompilerParams(vmem_limit_bytes=VMEM_LIMIT)
    vmem, smem = spec(pltpu.VMEM), spec(pltpu.SMEM)

    def call(kernel, name, ins, outs, scratch, *args):
        return pl.pallas_call(
            kernel,
            out_shape=tuple(jax.ShapeDtypeStruct(s, t) for s, t in outs),
            in_specs=ins,
            out_specs=(vmem,) * len(outs),
            scratch_shapes=scratch,
            compiler_params=params,
            name=name,
        )(*args)

    live = jnp.arange(slots, dtype=jnp.int32) < tile_count[0, 0]
    code = jnp.where(live, tile_rows[0, 0] + 4 * tile_cols[0, 0], -1)
    meta = jnp.pad(code.astype(F32), (0, TILE - slots))[None]

    near = jnp.concatenate([own, shift(own, "yh", 1)], axis=0)

    parcel = ((slots + 3, STRIP, TILE), BF)
    same, other = call(
        pack_kernel, "pack", [smem] + [vmem] * 3, [parcel] * 2, [], info, tile_values[0, 0], meta, cotangent[0]
    )
    strips = [same] + [shift(same if d == 2 else other, "x", d) for d in (1, 2, 3)]
    codes = jnp.stack([code] + [s[slots, 0, :slots].astype(jnp.int32) for s in strips[1:]])
    cots = [jnp.concatenate([s[slots + 1], s[slots + 2]], axis=1) for s in strips]
    column = lax.all_gather(near, Z, axis=0, tiled=True)

    listing = [pltpu.SMEM((3, 4 * slots + STEP), jnp.int32), pltpu.VMEM((4 * slots + 1, STRIP, TILE), BF)]
    parts = call(
        functools.partial(fwd_kernel, nz),
        "forward_tiles",
        [smem, smem] + [vmem] * 5,
        [((rows, feat), F32)] + [((rows, feat), BF)] * 3,
        listing + [pltpu.VMEM((16 * TILE, feat), F32)],
        codes, info, *strips, column,
    )

    back = [shift(parts[d], "x", -d) for d in (1, 2, 3)]
    block_sum = (parts[0] + (back[0].astype(F32) + back[1].astype(F32) + back[2].astype(F32))).astype(BF)
    core_cots = lax.all_gather(jnp.concatenate(cots, axis=0), "yl", axis=0, tiled=True)
    block_sum, core_cots = lax.optimization_barrier((block_sum, core_cots))
    pieces = lax.all_to_all(block_sum, COL, split_axis=0, concat_axis=0, tiled=True)
    agg = jnp.sum(pieces.reshape(col_devs, per_dev, feat).astype(F32), axis=0).astype(BF)
    group_agg = jnp.concatenate([agg] + [shift(agg, "x", d) for d in (1, 2, 3)], axis=0)
    other_cots = shift(core_cots, "core", 1)
    core_agg = lax.all_gather(group_agg, "yl", axis=0, tiled=True)
    other_agg = shift(core_agg, "core", 1)

    share = feat // col_devs
    chunk_rows = n_chunks * STRIP
    output_rows, keep, up, down, back = call(
        functools.partial(bwd_kernel, nz),
        "backward_tiles",
        [smem, smem] + [vmem] * 9,
        [((per_dev, feat), BF), ((chunk_rows + share, feat), F32)] + [((chunk_rows + 2 * share, feat), BF)] * 3,
        listing
        + [
            pltpu.VMEM((16 * TILE, feat), BF),
            pltpu.VMEM((16 * TILE, feat), BF),
            pltpu.VMEM((16 * TILE, feat), BF),
            pltpu.VMEM((groups * STRIP, feat), F32),
            pltpu.VMEM((4, feat, feat), F32),
            pltpu.VMEM((TILE, feat), F32),
        ],
        codes, info, *strips, core_agg, other_agg, core_cots, other_cots, weight,
    )
    (chunks,) = call(
        near_kernel,
        "near_sum",
        [vmem] * 4,
        [((n_chunks, STRIP + 2 * share, feat), BF)],
        [],
        keep, shift(up, Z, 1), shift(down, Z, -1), shift(back, Z, -2),
    )
    arrived = lax.all_to_all(chunks, ("yh", "za"), split_axis=0, concat_axis=0, tiled=True)
    node_total = per_dev * lax.axis_size(ROW) * col_devs
    grads, weight_part = call(
        functools.partial(far_kernel, node_total ** (-0.5)),
        "far_sum",
        [vmem],
        [((per_dev, feat), BF), ((share, feat), F32)],
        [],
        arrived,
    )
    grad_weight = lax.all_gather(weight_part, COL, axis=0, tiled=True)
    return output_rows[None], grads[None], grad_weight


def build(mesh, split):
    grid = Mesh(mesh.devices.reshape(split), NAMES)
    return jax.shard_map(
        on_device,
        mesh=grid,
        in_specs=(
            P(COL, ROW, None),
            P(),
            P(ROW, COL, None),
            P(ROW, COL, None, None, None),
            P(ROW, COL, None),
            P(ROW, COL, None),
            P(ROW, COL),
        ),
        out_specs=(P(ROW, COL, None), P(COL, ROW, None), P()),
        check_vma=False,
    )


def solution(mesh):
    return build(mesh, SPLIT)
```

```python
import functools

import jax
import jax.numpy as jnp
from jax import lax
from jax.experimental import pallas as pl
from jax.experimental.pallas import tpu as pltpu
from jax.sharding import Mesh
from jax.sharding import PartitionSpec as P

BF = jnp.bfloat16
F32 = jnp.float32
TILE = 128
STRIP = 64
SPLIT = (2, 3, 4, 4, 4, 2)
NAMES = ("yh", "za", "zb", "x", "yl", "core")
ROW = ("yh", "za", "zb", "x")
Z = ("za", "zb")
STEP = 4
LEFT = 16
COL = ("yl", "core")
VMEM_LIMIT = 40 * 1024 * 1024


def spec(space):
    return pl.BlockSpec(memory_space=space)


def pack_kernel(info, tiles, meta, cot, same, other):
    slots = tiles.shape[0]
    odd = info[0] == 1

    def one(s, carry):
        turned = tiles[s].T
        low, high = turned[:STRIP], turned[STRIP:]
        same[s] = jnp.where(odd, high, low)
        other[s] = jnp.where(odd, low, high)
        return carry

    lax.fori_loop(0, slots, one, 0, unroll=4)
    for ref in (same, other):
        ref[slots] = jnp.broadcast_to(meta[...], (STRIP, TILE)).astype(BF)
        ref[slots + 1] = cot[:, :TILE]
        ref[slots + 2] = cot[:, TILE:]


def live_list(codes, mine, row_of, place_of, table, strips, pool):
    slots = codes.shape[1]
    for j, ref in enumerate(strips):
        pool[j * slots : (j + 1) * slots] = ref[:slots]
    pool[4 * slots] = jnp.zeros((STRIP, TILE), BF)
    count = jnp.int32(0)
    for j in range(4):

        def one(s, n, j=j):
            code = codes[j, s]
            col, row = code >> 2, code & 3
            table[0, n] = j * slots + s
            table[1, n] = j * 4 + row_of(row)
            table[2, n] = place_of(col >> 1)
            return n + ((code >= 0) & ((col & 1) == mine)).astype(jnp.int32)

        count = lax.fori_loop(0, slots, one, count, unroll=4)
    for i in range(STEP):
        table[0, count + i] = 4 * slots
        table[1, count + i] = 0
        table[2, count + i] = 0
    return count


def fwd_kernel(nz, codes, info, s0, s1, s2, s3, feats, o0, o1, o2, o3, table, pool, acc):
    rows = o0.shape[0]
    mine, my_yh = info[1], info[2]

    def place_of(q):
        far = (q >= nz).astype(jnp.int32)
        return (q - far * nz) * 2 + (far ^ my_yh)

    count = live_list(codes, mine, lambda r: r, place_of, table, (s0, s1, s2, s3), pool)
    acc[...] = jnp.zeros_like(acc)

    def several(t, carry):
        terms = []
        for i in range(STEP):
            at = t * STEP + i
            block = feats[pl.ds(pl.multiple_of(table[2, at] * STRIP, STRIP), STRIP), :]
            term = lax.dot_general(
                pool[table[0, at]], block, (((0,), (0,)), ((), ())), preferred_element_type=F32
            )
            terms.append((pl.ds(pl.multiple_of(table[1, at] * TILE, TILE), TILE), term))
        for at, term in terms:
            acc[at, :] = acc[at, :] + term
        return carry

    lax.fori_loop(0, (count + (STEP - 1)) // STEP, several, 0)
    per = 4 * TILE
    for j, ref in enumerate((o0, o1, o2, o3)):
        ref[...] = acc[j * per : j * per + rows, :].astype(ref.dtype)


def bwd_kernel(
    nz, codes, info, s0, s1, s2, s3, r_own, r_other, lefts, w, out, keep, up, down, back,
    table, pool, agg, cots, ga, acc, gw4, act,
):
    rows, feat = 4 * TILE, w.shape[0]
    mine, col_pos, my_zb, my_x = info[1], info[3], info[4], info[5]
    my_yl, my_core = col_pos >> 1, col_pos & 1
    share = keep.shape[0] - (acc.shape[0] // 4)
    n_yl = rows // TILE
    count = live_list(codes, mine, lambda r: (my_yl - r) & (n_yl - 1), lambda q: q, table, (s0, s1, s2, s3), pool)
    acc[...] = jnp.zeros_like(acc)
    per = 4 * TILE
    for j in range(4):
        for d in range(n_yl):
            yl = (my_yl - d) & (n_yl - 1)
            base = yl * (r_own.shape[0] // n_yl) + j * STRIP
            n = STRIP if j < 3 else STRIP - LEFT
            for i, ref in enumerate((r_own, r_other)):
                to = pl.multiple_of(j * per + d * TILE + (my_core ^ i) * STRIP, STRIP)
                agg[pl.ds(to, STRIP), :] = ref[pl.ds(pl.multiple_of(base, LEFT), STRIP), :]
                cots[pl.ds(to, n), :] = ref[pl.ds(pl.multiple_of(base + 4 * STRIP, LEFT), n), :]
                if n < STRIP:
                    cots[pl.ds(pl.multiple_of(to + n, LEFT), LEFT), :] = lefts[yl * 2 + (my_core ^ i)]
        block = agg[j * per : j * per + rows, :]
        pre = jnp.dot(block, w[...], preferred_element_type=F32)
        sig = jax.nn.sigmoid(pre)
        if j == 0:
            act[...] = (pre * sig)[:TILE]
        slope = sig * (1.0 + pre * (1.0 - sig))
        gp = (cots[j * per : j * per + rows, :].astype(F32) * slope).astype(BF)
        gw4[(my_x - j) & 3] = lax.dot_general(block, gp, (((0,), (0,)), ((), ())), preferred_element_type=F32)
        ga[j * per : j * per + rows, :] = lax.dot_general(
            gp, w[...], (((1,), (1,)), ((), ())), preferred_element_type=F32
        ).astype(BF)
    out[...] = act[pl.ds(pl.multiple_of(my_core * STRIP, STRIP), STRIP), :].astype(BF)

    def several(t, carry):
        terms = []
        for i in range(STEP):
            at = t * STEP + i
            block = ga[pl.ds(pl.multiple_of(table[1, at] * TILE, TILE), TILE), :]
            term = jnp.dot(pool[table[0, at]], block, preferred_element_type=F32)
            terms.append((pl.ds(pl.multiple_of(table[2, at] * STRIP, STRIP), STRIP), term))
        for at, term in terms:
            acc[at, :] = acc[at, :] + term
        return carry

    lax.fori_loop(0, (count + (STEP - 1)) // STEP, several, 0)
    mine_rows = pl.ds(pl.multiple_of(col_pos * share, share), share)
    part = (gw4[0, mine_rows, :] + gw4[1, mine_rows, :]) + (gw4[2, mine_rows, :] + gw4[3, mine_rows, :])
    high = part.astype(BF)
    low = (part - high.astype(F32)).astype(BF)
    n_chunks = acc.shape[0] // (4 * STRIP)
    n_za = nz // 4
    for base, ref in ((0, keep), (1, up), (3, down), (2, back)):
        which = (my_zb + base) & 3
        for i in range(n_chunks):
            q = (i // n_za) * nz + 4 * (i % n_za) + which
            block = acc[pl.ds(pl.multiple_of(q * STRIP, STRIP), STRIP), :]
            ref[i * STRIP : (i + 1) * STRIP, :] = block.astype(ref.dtype)
    end = n_chunks * STRIP
    keep[end:, :] = part
    for ref in (up, down, back):
        ref[end : end + share, :] = high
        ref[end + share :, :] = low


def near_kernel(keep, up, down, back, chunks):
    n_chunks = chunks.shape[0]
    end = n_chunks * STRIP
    share = keep.shape[0] - end
    for i in range(n_chunks):
        at = slice(i * STRIP, (i + 1) * STRIP)
        chunks[i, :STRIP, :] = (
            (keep[at, :] + up[at, :].astype(F32)) + (down[at, :].astype(F32) + back[at, :].astype(F32))
        ).astype(BF)
    part = keep[end:, :]
    for ref in (up, down, back):
        part = part + (ref[end : end + share, :].astype(F32) + ref[end + share :, :].astype(F32))
    high = part.astype(BF)
    low = (part - high.astype(F32)).astype(BF)
    for i in range(n_chunks):
        chunks[i, STRIP : STRIP + share, :] = high
        chunks[i, STRIP + share :, :] = low


def far_kernel(scale, chunks, grads, weight_part):
    share = weight_part.shape[0]
    total = jnp.sum(chunks[...].astype(F32), axis=0)
    grads[...] = total[:STRIP].astype(BF)
    weight_part[...] = (total[STRIP : STRIP + share] + total[STRIP + share :]) * scale


def shift(value, axis, by):
    n = lax.axis_size(axis)
    return lax.ppermute(value, axis, [(i, (i + by) % n) for i in range(n)])


def on_device(features, weight, cotangent, tile_values, tile_rows, tile_cols, tile_count):
    own = features[0]
    per_dev, feat = own.shape
    slots = tile_values.shape[2]
    nz = lax.axis_size(Z)
    groups = 2 * nz
    n_chunks = groups // 4
    col_devs = lax.axis_size(COL)
    rows = per_dev * col_devs
    x = lax.axis_index("x")
    info = jnp.stack([x % 2, x // 2, lax.axis_index("yh"), lax.axis_index(COL), lax.axis_index("zb"), x]).astype(jnp.int32)
    params = pltpu.CompilerParams(vmem_limit_bytes=VMEM_LIMIT)
    vmem, smem = spec(pltpu.VMEM), spec(pltpu.SMEM)

    def call(kernel, name, ins, outs, scratch, *args):
        return pl.pallas_call(
            kernel,
            out_shape=tuple(jax.ShapeDtypeStruct(s, t) for s, t in outs),
            in_specs=ins,
            out_specs=(vmem,) * len(outs),
            scratch_shapes=scratch,
            compiler_params=params,
            name=name,
        )(*args)

    live = jnp.arange(slots, dtype=jnp.int32) < tile_count[0, 0]
    code = jnp.where(live, tile_rows[0, 0] + 4 * tile_cols[0, 0], -1)
    meta = jnp.pad(code.astype(F32), (0, TILE - slots))[None]

    near = jnp.concatenate([own, shift(own, "yh", 1)], axis=0)

    parcel = ((slots + 3, STRIP, TILE), BF)
    same, other = call(
        pack_kernel, "pack", [smem] + [vmem] * 3, [parcel] * 2, [], info, tile_values[0, 0], meta, cotangent[0]
    )
    strips = [same] + [shift(same if d == 2 else other, "x", d) for d in (1, 2, 3)]
    codes = jnp.stack([code] + [s[slots, 0, :slots].astype(jnp.int32) for s in strips[1:]])
    cots = [jnp.concatenate([s[slots + 1], s[slots + 2]], axis=1) for s in strips]
    column = lax.all_gather(near, Z, axis=0, tiled=True)

    listing = [pltpu.SMEM((3, 4 * slots + STEP), jnp.int32), pltpu.VMEM((4 * slots + 1, STRIP, TILE), BF)]
    parts = call(
        functools.partial(fwd_kernel, nz),
        "forward_tiles",
        [smem, smem] + [vmem] * 5,
        [((rows, feat), F32)] + [((rows, feat), BF)] * 3,
        listing + [pltpu.VMEM((16 * TILE, feat), F32)],
        codes, info, *strips, column,
    )

    back = [shift(parts[d], "x", -d) for d in (1, 2, 3)]
    block_sum = (parts[0] + (back[0].astype(F32) + back[1].astype(F32) + back[2].astype(F32))).astype(BF)
    cot_rows = jnp.concatenate(cots, axis=0)
    left = jnp.broadcast_to(cot_rows[4 * STRIP - LEFT :][None], (col_devs, LEFT, feat))
    sent = jnp.concatenate([block_sum.reshape(col_devs, per_dev, feat), left], axis=1)
    pieces = lax.all_to_all(sent, COL, split_axis=0, concat_axis=0, tiled=True)
    agg = jnp.sum(pieces[:, :per_dev].astype(F32), axis=0).astype(BF)
    lefts = pieces[:, per_dev:]
    group_agg = [agg] + [shift(agg, "x", d) for d in (1, 2, 3)]
    group_rows = jnp.concatenate(group_agg + [cot_rows[: 4 * STRIP - LEFT]], axis=0)
    core_rows = lax.all_gather(group_rows, "yl", axis=0, tiled=True)
    other_rows = shift(core_rows, "core", 1)

    share = feat // col_devs
    chunk_rows = n_chunks * STRIP
    output_rows, keep, up, down, back = call(
        functools.partial(bwd_kernel, nz),
        "backward_tiles",
        [smem, smem] + [vmem] * 8,
        [((per_dev, feat), BF), ((chunk_rows + share, feat), F32)] + [((chunk_rows + 2 * share, feat), BF)] * 3,
        listing
        + [
            pltpu.VMEM((16 * TILE, feat), BF),
            pltpu.VMEM((16 * TILE, feat), BF),
            pltpu.VMEM((16 * TILE, feat), BF),
            pltpu.VMEM((groups * STRIP, feat), F32),
            pltpu.VMEM((4, feat, feat), F32),
            pltpu.VMEM((TILE, feat), F32),
        ],
        codes, info, *strips, core_rows, other_rows, lefts, weight,
    )
    (chunks,) = call(
        near_kernel,
        "near_sum",
        [vmem] * 4,
        [((n_chunks, STRIP + 2 * share, feat), BF)],
        [],
        keep, shift(up, Z, 1), shift(down, Z, -1), shift(back, Z, -2),
    )
    arrived = lax.all_to_all(chunks, ("yh", "za"), split_axis=0, concat_axis=0, tiled=True)
    node_total = per_dev * lax.axis_size(ROW) * col_devs
    grads, weight_part = call(
        functools.partial(far_kernel, node_total ** (-0.5)),
        "far_sum",
        [vmem],
        [((per_dev, feat), BF), ((share, feat), F32)],
        [],
        arrived,
    )
    grad_weight = lax.all_gather(weight_part, COL, axis=0, tiled=True)
    return output_rows[None], grads[None], grad_weight


def build(mesh, split):
    grid = Mesh(mesh.devices.reshape(split), NAMES)
    return jax.shard_map(
        on_device,
        mesh=grid,
        in_specs=(
            P(COL, ROW, None),
            P(),
            P(ROW, COL, None),
            P(ROW, COL, None, None, None),
            P(ROW, COL, None),
            P(ROW, COL, None),
            P(ROW, COL),
        ),
        out_specs=(P(ROW, COL, None), P(COL, ROW, None), P()),
        check_vma=False,
    )


def solution(mesh):
    return build(mesh, SPLIT)
```

```python
import functools

import jax
import jax.numpy as jnp
from jax import lax
from jax.experimental import pallas as pl
from jax.experimental.pallas import tpu as pltpu
from jax.sharding import Mesh
from jax.sharding import PartitionSpec as P

BF = jnp.bfloat16
F32 = jnp.float32
TILE = 128
STRIP = 64
SPLIT = (2, 3, 4, 4, 4, 2)
NAMES = ("yh", "za", "zb", "x", "yl", "core")
ROW = ("yh", "za", "zb", "x")
Z = ("za", "zb")
STEP = 4
LEFT = 16
COL = ("yl", "core")
VMEM_LIMIT = 40 * 1024 * 1024


def spec(space):
    return pl.BlockSpec(memory_space=space)


def pack_kernel(info, tiles, meta, cot, same, other):
    slots = tiles.shape[0]
    odd = info[0] == 1

    def one(s, carry):
        turned = tiles[s].T
        low, high = turned[:STRIP], turned[STRIP:]
        same[s] = jnp.where(odd, high, low)
        other[s] = jnp.where(odd, low, high)
        return carry

    lax.fori_loop(0, slots, one, 0, unroll=4)
    for ref in (same, other):
        ref[slots] = jnp.broadcast_to(meta[...], (STRIP, TILE)).astype(BF)
        ref[slots + 1] = cot[:, :TILE]
        ref[slots + 2] = cot[:, TILE:]


def live_list(codes, mine, row_of, place_of, table, strips, pool):
    slots = codes.shape[1]
    for j, ref in enumerate(strips):
        pool[j * slots : (j + 1) * slots] = ref[:slots]
    pool[4 * slots] = jnp.zeros((STRIP, TILE), BF)
    count = jnp.int32(0)
    for j in range(4):

        def one(s, n, j=j):
            code = codes[j, s]
            col, row = code >> 2, code & 3
            table[0, n] = j * slots + s
            table[1, n] = j * 4 + row_of(row)
            table[2, n] = place_of(col >> 1)
            return n + ((code >= 0) & ((col & 1) == mine)).astype(jnp.int32)

        count = lax.fori_loop(0, slots, one, count, unroll=4)
    for i in range(STEP):
        table[0, count + i] = 4 * slots
        table[1, count + i] = 0
        table[2, count + i] = 0
    return count


def fwd_kernel(nz, codes, info, s0, s1, s2, s3, feats, o0, o1, o2, o3, table, pool, acc):
    rows = o0.shape[0]
    mine, my_yh = info[1], info[2]

    def place_of(q):
        far = (q >= nz).astype(jnp.int32)
        return (q - far * nz) * 2 + (far ^ my_yh)

    count = live_list(codes, mine, lambda r: r, place_of, table, (s0, s1, s2, s3), pool)
    acc[...] = jnp.zeros_like(acc)

    def several(t, carry):
        terms = []
        for i in range(STEP):
            at = t * STEP + i
            block = feats[pl.ds(pl.multiple_of(table[2, at] * STRIP, STRIP), STRIP), :]
            term = lax.dot_general(
                pool[table[0, at]], block, (((0,), (0,)), ((), ())), preferred_element_type=F32
            )
            terms.append((pl.ds(pl.multiple_of(table[1, at] * TILE, TILE), TILE), term))
        for at, term in terms:
            acc[at, :] = acc[at, :] + term
        return carry

    lax.fori_loop(0, (count + (STEP - 1)) // STEP, several, 0)
    per = 4 * TILE
    for j, ref in enumerate((o0, o1, o2, o3)):
        ref[...] = acc[j * per : j * per + rows, :].astype(ref.dtype)


def bwd_kernel(
    nz, codes, info, s0, s1, s2, s3, r_own, r_other, lefts, w, out, keep, up, down, fore, back,
    table, pool, agg, cots, ga, acc, gw4, act,
):
    rows, feat = 4 * TILE, w.shape[0]
    mine, col_pos, my_zb, my_x = info[1], info[3], info[4], info[5]
    my_yl, my_core = col_pos >> 1, col_pos & 1
    share = keep.shape[0] - (acc.shape[0] // 4)
    n_yl = rows // TILE
    count = live_list(codes, mine, lambda r: (my_yl - r) & (n_yl - 1), lambda q: q, table, (s0, s1, s2, s3), pool)
    acc[...] = jnp.zeros_like(acc)
    per = 4 * TILE
    for j in range(4):
        for d in range(n_yl):
            yl = (my_yl - d) & (n_yl - 1)
            base = yl * (r_own.shape[0] // n_yl) + j * STRIP
            n = STRIP if j < 3 else STRIP - LEFT
            for i, ref in enumerate((r_own, r_other)):
                to = pl.multiple_of(j * per + d * TILE + (my_core ^ i) * STRIP, STRIP)
                agg[pl.ds(to, STRIP), :] = ref[pl.ds(pl.multiple_of(base, LEFT), STRIP), :]
                cots[pl.ds(to, n), :] = ref[pl.ds(pl.multiple_of(base + 4 * STRIP, LEFT), n), :]
                if n < STRIP:
                    cots[pl.ds(pl.multiple_of(to + n, LEFT), LEFT), :] = lefts[yl * 2 + (my_core ^ i)]
        block = agg[j * per : j * per + rows, :]
        pre = jnp.dot(block, w[...], preferred_element_type=F32)
        sig = jax.nn.sigmoid(pre)
        if j == 0:
            act[...] = (pre * sig)[:TILE]
        slope = sig * (1.0 + pre * (1.0 - sig))
        gp = (cots[j * per : j * per + rows, :].astype(F32) * slope).astype(BF)
        gw4[(my_x - j) & 3] = lax.dot_general(block, gp, (((0,), (0,)), ((), ())), preferred_element_type=F32)
        ga[j * per : j * per + rows, :] = lax.dot_general(
            gp, w[...], (((1,), (1,)), ((), ())), preferred_element_type=F32
        ).astype(BF)
    out[...] = act[pl.ds(pl.multiple_of(my_core * STRIP, STRIP), STRIP), :].astype(BF)

    def several(t, carry):
        terms = []
        for i in range(STEP):
            at = t * STEP + i
            block = ga[pl.ds(pl.multiple_of(table[1, at] * TILE, TILE), TILE), :]
            term = jnp.dot(pool[table[0, at]], block, preferred_element_type=F32)
            terms.append((pl.ds(pl.multiple_of(table[2, at] * STRIP, STRIP), STRIP), term))
        for at, term in terms:
            acc[at, :] = acc[at, :] + term
        return carry

    lax.fori_loop(0, (count + (STEP - 1)) // STEP, several, 0)
    mine_rows = pl.ds(pl.multiple_of(col_pos * share, share), share)
    part = (gw4[0, mine_rows, :] + gw4[1, mine_rows, :]) + (gw4[2, mine_rows, :] + gw4[3, mine_rows, :])
    high = part.astype(BF)
    low = (part - high.astype(F32)).astype(BF)
    n_chunks = acc.shape[0] // (4 * STRIP)
    n_za = nz // 4
    half = n_chunks // 2
    whole = range(n_chunks)
    for base, ref, these in ((0, keep, whole), (1, up, whole), (3, down, whole), (2, back, whole[:half]), (2, fore, whole[half:])):
        which = (my_zb + base) & 3
        for place, i in enumerate(these):
            q = (i // n_za) * nz + 4 * (i % n_za) + which
            block = acc[pl.ds(pl.multiple_of(q * STRIP, STRIP), STRIP), :]
            ref[place * STRIP : (place + 1) * STRIP, :] = block.astype(ref.dtype)
    end = n_chunks * STRIP
    keep[end:, :] = part
    for ref, end in ((up, end), (down, end), (back, half * STRIP)):
        ref[end : end + share, :] = high
        ref[end + share :, :] = low


def near_kernel(keep, up, down, fore, back, chunks):
    n_chunks = chunks.shape[0]
    half = n_chunks // 2
    end = n_chunks * STRIP
    share = keep.shape[0] - end
    for i in range(n_chunks):
        at = slice(i * STRIP, (i + 1) * STRIP)
        far, j = (back, i) if i < half else (fore, i - half)
        away = far[j * STRIP : (j + 1) * STRIP, :].astype(F32)
        total = (keep[at, :] + up[at, :].astype(F32)) + (down[at, :].astype(F32) + away)
        chunks[i, :STRIP, :] = total.astype(BF)
    part = keep[end:, :]
    for ref, at in ((up, end), (down, end), (back, half * STRIP)):
        part = part + (ref[at : at + share, :].astype(F32) + ref[at + share :, :].astype(F32))
    high = part.astype(BF)
    low = (part - high.astype(F32)).astype(BF)
    for i in range(n_chunks):
        chunks[i, STRIP : STRIP + share, :] = high
        chunks[i, STRIP + share :, :] = low


def far_kernel(scale, chunks, grads, weight_part):
    share = weight_part.shape[0]
    total = jnp.sum(chunks[...].astype(F32), axis=0)
    grads[...] = total[:STRIP].astype(BF)
    weight_part[...] = (total[STRIP : STRIP + share] + total[STRIP + share :]) * scale


def shift(value, axis, by):
    n = lax.axis_size(axis)
    return lax.ppermute(value, axis, [(i, (i + by) % n) for i in range(n)])


def on_device(features, weight, cotangent, tile_values, tile_rows, tile_cols, tile_count):
    own = features[0]
    per_dev, feat = own.shape
    slots = tile_values.shape[2]
    nz = lax.axis_size(Z)
    groups = 2 * nz
    n_chunks = groups // 4
    col_devs = lax.axis_size(COL)
    rows = per_dev * col_devs
    x = lax.axis_index("x")
    info = jnp.stack([x % 2, x // 2, lax.axis_index("yh"), lax.axis_index(COL), lax.axis_index("zb"), x]).astype(jnp.int32)
    params = pltpu.CompilerParams(vmem_limit_bytes=VMEM_LIMIT)
    vmem, smem = spec(pltpu.VMEM), spec(pltpu.SMEM)

    def call(kernel, name, ins, outs, scratch, *args):
        return pl.pallas_call(
            kernel,
            out_shape=tuple(jax.ShapeDtypeStruct(s, t) for s, t in outs),
            in_specs=ins,
            out_specs=(vmem,) * len(outs),
            scratch_shapes=scratch,
            compiler_params=params,
            name=name,
        )(*args)

    live = jnp.arange(slots, dtype=jnp.int32) < tile_count[0, 0]
    code = jnp.where(live, tile_rows[0, 0] + 4 * tile_cols[0, 0], -1)
    meta = jnp.pad(code.astype(F32), (0, TILE - slots))[None]

    near = jnp.concatenate([own, shift(own, "yh", 1)], axis=0)

    parcel = ((slots + 3, STRIP, TILE), BF)
    same, other = call(
        pack_kernel, "pack", [smem] + [vmem] * 3, [parcel] * 2, [], info, tile_values[0, 0], meta, cotangent[0]
    )
    strips = [same] + [shift(same if d == 2 else other, "x", d) for d in (1, 2, 3)]
    codes = jnp.stack([code] + [s[slots, 0, :slots].astype(jnp.int32) for s in strips[1:]])
    cots = [jnp.concatenate([s[slots + 1], s[slots + 2]], axis=1) for s in strips]
    column = lax.all_gather(near, Z, axis=0, tiled=True)

    listing = [pltpu.SMEM((3, 4 * slots + STEP), jnp.int32), pltpu.VMEM((4 * slots + 1, STRIP, TILE), BF)]
    parts = call(
        functools.partial(fwd_kernel, nz),
        "forward_tiles",
        [smem, smem] + [vmem] * 5,
        [((rows, feat), F32)] + [((rows, feat), BF)] * 3,
        listing + [pltpu.VMEM((16 * TILE, feat), F32)],
        codes, info, *strips, column,
    )

    back = [shift(parts[d], "x", -d) for d in (2, 1, 3)]
    block_sum = (parts[0] + (back[0].astype(F32) + back[1].astype(F32) + back[2].astype(F32))).astype(BF)
    cot_rows = jnp.concatenate(cots, axis=0)
    left = jnp.broadcast_to(cot_rows[4 * STRIP - LEFT :][None], (col_devs, LEFT, feat))
    sent = jnp.concatenate([block_sum.reshape(col_devs, per_dev, feat), left], axis=1)
    pieces = lax.all_to_all(sent, COL, split_axis=0, concat_axis=0, tiled=True)
    agg = jnp.sum(pieces[:, :per_dev].astype(F32), axis=0).astype(BF)
    lefts = pieces[:, per_dev:]
    group_agg = [agg] + [shift(agg, "x", d) for d in (1, 2, 3)]
    group_rows = jnp.concatenate(group_agg + [cot_rows[: 4 * STRIP - LEFT]], axis=0)
    core_rows = lax.all_gather(group_rows, "yl", axis=0, tiled=True)
    other_rows = shift(core_rows, "core", 1)

    share = feat // col_devs
    chunk_rows = n_chunks * STRIP
    output_rows, keep, up, down, fore, back = call(
        functools.partial(bwd_kernel, nz),
        "backward_tiles",
        [smem, smem] + [vmem] * 8,
        [((per_dev, feat), BF), ((chunk_rows + share, feat), F32)] + [((chunk_rows + 2 * share, feat), BF)] * 2
        + [((chunk_rows // 2, feat), BF), ((chunk_rows // 2 + 2 * share, feat), BF)],
        listing
        + [
            pltpu.VMEM((16 * TILE, feat), BF),
            pltpu.VMEM((16 * TILE, feat), BF),
            pltpu.VMEM((16 * TILE, feat), BF),
            pltpu.VMEM((groups * STRIP, feat), F32),
            pltpu.VMEM((4, feat, feat), F32),
            pltpu.VMEM((TILE, feat), F32),
        ],
        codes, info, *strips, core_rows, other_rows, lefts, weight,
    )
    back, fore = shift(back, Z, -2), shift(fore, Z, 2)
    (chunks,) = call(
        near_kernel,
        "near_sum",
        [vmem] * 5,
        [((n_chunks, STRIP + 2 * share, feat), BF)],
        [],
        keep, shift(up, Z, 1), shift(down, Z, -1), fore, back,
    )
    arrived = lax.all_to_all(chunks, ("yh", "za"), split_axis=0, concat_axis=0, tiled=True)
    node_total = per_dev * lax.axis_size(ROW) * col_devs
    grads, weight_part = call(
        functools.partial(far_kernel, node_total ** (-0.5)),
        "far_sum",
        [vmem],
        [((per_dev, feat), BF), ((share, feat), F32)],
        [],
        arrived,
    )
    grad_weight = lax.all_gather(weight_part, COL, axis=0, tiled=True)
    return output_rows[None], grads[None], grad_weight


def build(mesh, split):
    grid = Mesh(mesh.devices.reshape(split), NAMES)
    return jax.shard_map(
        on_device,
        mesh=grid,
        in_specs=(
            P(COL, ROW, None),
            P(),
            P(ROW, COL, None),
            P(ROW, COL, None, None, None),
            P(ROW, COL, None),
            P(ROW, COL, None),
            P(ROW, COL),
        ),
        out_specs=(P(ROW, COL, None), P(COL, ROW, None), P()),
        check_vma=False,
    )


def solution(mesh):
    return build(mesh, SPLIT)
```

```python
import functools

import jax
import jax.numpy as jnp
from jax import lax
from jax.experimental import pallas as pl
from jax.experimental.pallas import tpu as pltpu
from jax.sharding import Mesh
from jax.sharding import PartitionSpec as P

BF = jnp.bfloat16
F32 = jnp.float32
TILE = 128
STRIP = 64
SPLIT = (2, 3, 4, 4, 4, 2)
NAMES = ("yh", "za", "zb", "x", "yl", "core")
ROW = ("yh", "za", "zb", "x")
Z = ("za", "zb")
STEP = 4
LEFT = 16
COL = ("yl", "core")
VMEM_LIMIT = 40 * 1024 * 1024


def spec(space):
    return pl.BlockSpec(memory_space=space)


def pack_kernel(info, tiles, meta, cot, same, other):
    slots = tiles.shape[0]
    odd = info[0] == 1

    def one(s, carry):
        turned = tiles[s].T
        low, high = turned[:STRIP], turned[STRIP:]
        same[s] = jnp.where(odd, high, low)
        other[s] = jnp.where(odd, low, high)
        return carry

    lax.fori_loop(0, slots, one, 0, unroll=4)
    for ref in (same, other):
        ref[slots] = jnp.broadcast_to(meta[...], (STRIP, TILE)).astype(BF)
        ref[slots + 1] = cot[:, :TILE]
        ref[slots + 2] = cot[:, TILE:]


def live_list(codes, mine, row_of, place_of, table, strips, pool):
    slots = codes.shape[1]
    for j, ref in enumerate(strips):
        pool[j * slots : (j + 1) * slots] = ref[:slots]
    pool[4 * slots] = jnp.zeros((STRIP, TILE), BF)
    count = jnp.int32(0)
    for j in range(4):

        def one(s, n, j=j):
            code = codes[j, s]
            col, row = code >> 2, code & 3
            table[0, n] = j * slots + s
            table[1, n] = j * 4 + row_of(row)
            table[2, n] = place_of(col >> 1)
            return n + ((code >= 0) & ((col & 1) == mine)).astype(jnp.int32)

        count = lax.fori_loop(0, slots, one, count, unroll=4)
    for i in range(STEP):
        table[0, count + i] = 4 * slots
        table[1, count + i] = 0
        table[2, count + i] = 0
    return count


def fwd_kernel(nz, codes, info, s0, s1, s2, s3, feats, o0, o1, o2, o3, table, pool, acc):
    rows = o0.shape[0]
    mine, my_yh = info[1], info[2]

    def place_of(q):
        far = (q >= nz).astype(jnp.int32)
        return (q - far * nz) * 2 + (far ^ my_yh)

    count = live_list(codes, mine, lambda r: r, place_of, table, (s0, s1, s2, s3), pool)
    acc[...] = jnp.zeros_like(acc)

    def several(t, carry):
        terms = []
        for i in range(STEP):
            at = t * STEP + i
            block = feats[pl.ds(pl.multiple_of(table[2, at] * STRIP, STRIP), STRIP), :]
            term = lax.dot_general(
                pool[table[0, at]], block, (((0,), (0,)), ((), ())), preferred_element_type=F32
            )
            terms.append((pl.ds(pl.multiple_of(table[1, at] * TILE, TILE), TILE), term))
        for at, term in terms:
            acc[at, :] = acc[at, :] + term
        return carry

    lax.fori_loop(0, (count + (STEP - 1)) // STEP, several, 0)
    per = 4 * TILE
    for j, ref in enumerate((o0, o1, o2, o3)):
        ref[...] = acc[j * per : j * per + rows, :].astype(ref.dtype)


def bwd_kernel(
    nz, codes, info, s0, s1, s2, s3, r_own, r_other, lefts, w, out, keep, up, down, fore, back,
    table, pool, agg, cots, ga, acc, gw4, act,
):
    rows, feat = 4 * TILE, w.shape[0]
    mine, col_pos, my_zb, my_x = info[1], info[3], info[4], info[5]
    my_yl, my_core = col_pos >> 1, col_pos & 1
    share = keep.shape[0] - (acc.shape[0] // 4)
    n_yl = rows // TILE
    count = live_list(codes, mine, lambda r: (my_yl - r) & (n_yl - 1), lambda q: q, table, (s0, s1, s2, s3), pool)
    acc[...] = jnp.zeros_like(acc)
    per = 4 * TILE
    for j in range(4):
        for d in range(n_yl):
            yl = (my_yl - d) & (n_yl - 1)
            base = yl * (r_own.shape[0] // n_yl) + j * STRIP
            n = STRIP if j < 3 else STRIP - LEFT
            for i, ref in enumerate((r_own, r_other)):
                to = pl.multiple_of(j * per + d * TILE + (my_core ^ i) * STRIP, STRIP)
                agg[pl.ds(to, STRIP), :] = ref[pl.ds(pl.multiple_of(base, LEFT), STRIP), :]
                cots[pl.ds(to, n), :] = ref[pl.ds(pl.multiple_of(base + 4 * STRIP, LEFT), n), :]
                if n < STRIP:
                    cots[pl.ds(pl.multiple_of(to + n, LEFT), LEFT), :] = lefts[yl * 2 + (my_core ^ i)]
        block = agg[j * per : j * per + rows, :]
        pre = jnp.dot(block, w[...], preferred_element_type=F32)
        sig = jax.nn.sigmoid(pre)
        if j == 0:
            act[...] = (pre * sig)[:TILE]
        slope = sig * (1.0 + pre * (1.0 - sig))
        gp = (cots[j * per : j * per + rows, :].astype(F32) * slope).astype(BF)
        gw4[(my_x - j) & 3] = lax.dot_general(block, gp, (((0,), (0,)), ((), ())), preferred_element_type=F32)
        ga[j * per : j * per + rows, :] = lax.dot_general(
            gp, w[...], (((1,), (1,)), ((), ())), preferred_element_type=F32
        ).astype(BF)
    out[...] = act[pl.ds(pl.multiple_of(my_core * STRIP, STRIP), STRIP), :].astype(BF)

    def several(t, carry):
        terms = []
        for i in range(STEP):
            at = t * STEP + i
            block = ga[pl.ds(pl.multiple_of(table[1, at] * TILE, TILE), TILE), :]
            term = jnp.dot(pool[table[0, at]], block, preferred_element_type=F32)
            terms.append((pl.ds(pl.multiple_of(table[2, at] * STRIP, STRIP), STRIP), term))
        for at, term in terms:
            acc[at, :] = acc[at, :] + term
        return carry

    lax.fori_loop(0, (count + (STEP - 1)) // STEP, several, 0)
    mine_rows = pl.ds(pl.multiple_of(col_pos * share, share), share)
    part = (gw4[0, mine_rows, :] + gw4[1, mine_rows, :]) + (gw4[2, mine_rows, :] + gw4[3, mine_rows, :])
    high = part.astype(BF)
    low = (part - high.astype(F32)).astype(BF)
    n_chunks = acc.shape[0] // (4 * STRIP)
    n_za = nz // 4
    half = n_chunks // 2
    whole = range(n_chunks)
    for base, ref, these in ((0, keep, whole), (1, up, whole), (3, down, whole), (2, back, whole[:half]), (2, fore, whole[half:])):
        which = (my_zb + base) & 3
        for place, i in enumerate(these):
            q = (i // n_za) * nz + 4 * (i % n_za) + which
            block = acc[pl.ds(pl.multiple_of(q * STRIP, STRIP), STRIP), :]
            ref[place * STRIP : (place + 1) * STRIP, :] = block.astype(ref.dtype)
    end = n_chunks * STRIP
    keep[end:, :] = part
    for ref, end in ((up, end), (down, end), (back, half * STRIP)):
        ref[end : end + share, :] = high
        ref[end + share :, :] = low


def near_kernel(keep, up, down, fore, back, chunks):
    n_chunks = chunks.shape[0]
    half = n_chunks // 2
    end = n_chunks * STRIP
    share = keep.shape[0] - end
    for i in range(n_chunks):
        at = slice(i * STRIP, (i + 1) * STRIP)
        far, j = (back, i) if i < half else (fore, i - half)
        away = far[j * STRIP : (j + 1) * STRIP, :].astype(F32)
        total = (keep[at, :] + up[at, :].astype(F32)) + (down[at, :].astype(F32) + away)
        chunks[i, :STRIP, :] = total.astype(BF)
    part = keep[end:, :]
    for ref, at in ((up, end), (down, end), (back, half * STRIP)):
        part = part + (ref[at : at + share, :].astype(F32) + ref[at + share :, :].astype(F32))
    high = part.astype(BF)
    low = (part - high.astype(F32)).astype(BF)
    for i in range(n_chunks):
        chunks[i, STRIP : STRIP + share, :] = high
        chunks[i, STRIP + share :, :] = low


def far_kernel(scale, chunks, grads, weight_part):
    share = weight_part.shape[0]
    total = jnp.sum(chunks[...].astype(F32), axis=0)
    grads[...] = total[:STRIP].astype(BF)
    weight_part[...] = (total[STRIP : STRIP + share] + total[STRIP + share :]) * scale


def shift(value, axis, by):
    n = lax.axis_size(axis)
    return lax.ppermute(value, axis, [(i, (i + by) % n) for i in range(n)])


def on_device(features, weight, cotangent, tile_values, tile_rows, tile_cols, tile_count):
    own = features[0]
    per_dev, feat = own.shape
    slots = tile_values.shape[2]
    nz = lax.axis_size(Z)
    groups = 2 * nz
    n_chunks = groups // 4
    col_devs = lax.axis_size(COL)
    rows = per_dev * col_devs
    x = lax.axis_index("x")
    info = jnp.stack([x % 2, x // 2, lax.axis_index("yh"), lax.axis_index(COL), lax.axis_index("zb"), x]).astype(jnp.int32)
    params = pltpu.CompilerParams(vmem_limit_bytes=VMEM_LIMIT)
    vmem, smem = spec(pltpu.VMEM), spec(pltpu.SMEM)

    def call(kernel, name, ins, outs, scratch, *args):
        return pl.pallas_call(
            kernel,
            out_shape=tuple(jax.ShapeDtypeStruct(s, t) for s, t in outs),
            in_specs=ins,
            out_specs=(vmem,) * len(outs),
            scratch_shapes=scratch,
            compiler_params=params,
            name=name,
        )(*args)

    live = jnp.arange(slots, dtype=jnp.int32) < tile_count[0, 0]
    code = jnp.where(live, tile_rows[0, 0] + 4 * tile_cols[0, 0], -1)
    meta = jnp.pad(code.astype(F32), (0, TILE - slots))[None]

    facing, meta = lax.optimization_barrier((shift(own, "yh", 1), meta))
    near = jnp.concatenate([own, facing], axis=0)

    parcel = ((slots + 3, STRIP, TILE), BF)
    same, other = call(
        pack_kernel, "pack", [smem] + [vmem] * 3, [parcel] * 2, [], info, tile_values[0, 0], meta, cotangent[0]
    )
    strips = [same] + [shift(same if d == 2 else other, "x", d) for d in (1, 2, 3)]
    codes = jnp.stack([code] + [s[slots, 0, :slots].astype(jnp.int32) for s in strips[1:]])
    cots = [jnp.concatenate([s[slots + 1], s[slots + 2]], axis=1) for s in strips]
    column = lax.all_gather(near, Z, axis=0, tiled=True)

    listing = [pltpu.SMEM((3, 4 * slots + STEP), jnp.int32), pltpu.VMEM((4 * slots + 1, STRIP, TILE), BF)]
    parts = call(
        functools.partial(fwd_kernel, nz),
        "forward_tiles",
        [smem, smem] + [vmem] * 5,
        [((rows, feat), F32)] + [((rows, feat), BF)] * 3,
        listing + [pltpu.VMEM((16 * TILE, feat), F32)],
        codes, info, *strips, column,
    )

    back = [shift(parts[d], "x", -d) for d in (2, 1, 3)]
    block_sum = (parts[0] + (back[0].astype(F32) + back[1].astype(F32) + back[2].astype(F32))).astype(BF)
    cot_rows = jnp.concatenate(cots, axis=0)
    left = jnp.broadcast_to(cot_rows[4 * STRIP - LEFT :][None], (col_devs, LEFT, feat))
    sent = jnp.concatenate([block_sum.reshape(col_devs, per_dev, feat), left], axis=1)
    pieces = lax.all_to_all(sent, COL, split_axis=0, concat_axis=0, tiled=True)
    agg = jnp.sum(pieces[:, :per_dev].astype(F32), axis=0).astype(BF)
    lefts = pieces[:, per_dev:]
    group_agg = [agg] + [shift(agg, "x", d) for d in (1, 2, 3)]
    group_rows = jnp.concatenate(group_agg + [cot_rows[: 4 * STRIP - LEFT]], axis=0)
    core_rows = lax.all_gather(group_rows, "yl", axis=0, tiled=True)
    other_rows = shift(core_rows, "core", 1)

    share = feat // col_devs
    chunk_rows = n_chunks * STRIP
    output_rows, keep, up, down, fore, back = call(
        functools.partial(bwd_kernel, nz),
        "backward_tiles",
        [smem, smem] + [vmem] * 8,
        [((per_dev, feat), BF), ((chunk_rows + share, feat), F32)] + [((chunk_rows + 2 * share, feat), BF)] * 2
        + [((chunk_rows // 2, feat), BF), ((chunk_rows // 2 + 2 * share, feat), BF)],
        listing
        + [
            pltpu.VMEM((16 * TILE, feat), BF),
            pltpu.VMEM((16 * TILE, feat), BF),
            pltpu.VMEM((16 * TILE, feat), BF),
            pltpu.VMEM((groups * STRIP, feat), F32),
            pltpu.VMEM((4, feat, feat), F32),
            pltpu.VMEM((TILE, feat), F32),
        ],
        codes, info, *strips, core_rows, other_rows, lefts, weight,
    )
    back, fore = shift(back, Z, -2), shift(fore, Z, 2)
    (chunks,) = call(
        near_kernel,
        "near_sum",
        [vmem] * 5,
        [((n_chunks, STRIP + 2 * share, feat), BF)],
        [],
        keep, shift(up, Z, 1), shift(down, Z, -1), fore, back,
    )
    arrived = lax.all_to_all(chunks, ("yh", "za"), split_axis=0, concat_axis=0, tiled=True)
    node_total = per_dev * lax.axis_size(ROW) * col_devs
    grads, weight_part = call(
        functools.partial(far_kernel, node_total ** (-0.5)),
        "far_sum",
        [vmem],
        [((per_dev, feat), BF), ((share, feat), F32)],
        [],
        arrived,
    )
    grad_weight = lax.all_gather(weight_part, COL, axis=0, tiled=True)
    return output_rows[None], grads[None], grad_weight


def build(mesh, split):
    grid = Mesh(mesh.devices.reshape(split), NAMES)
    return jax.shard_map(
        on_device,
        mesh=grid,
        in_specs=(
            P(COL, ROW, None),
            P(),
            P(ROW, COL, None),
            P(ROW, COL, None, None, None),
            P(ROW, COL, None),
            P(ROW, COL, None),
            P(ROW, COL),
        ),
        out_specs=(P(ROW, COL, None), P(COL, ROW, None), P()),
        check_vma=False,
    )


def solution(mesh):
    return build(mesh, SPLIT)
```
